32 devices in a mesh: space: 8 (over z, x), var: 4 (over y, core).
Axes of the slice: x: 2, y: 2, z: 4, core: 2. Of those that a mesh axis runs over, the one named last changes fastest.
Arguments:
- control: bfloat16 [8192, 1536], P('space', 'var'), may hold values from -6 to 6
- roots: bfloat16 [64, 5, 128, 128], P('space'), may hold values from -0.25 to 0.25
- neighbours: int32 [64, 5], P('space'), may hold values from 0 to 63, as said below
- sigma: float32 [96, 8192], P('var', 'space'), may hold values from 0.3 to 3
- obs_op: bfloat16 [96, 16], P('var'), may hold values from -0.625 to 0.625
- foot_cols: int32 [256, 16], P('space'), may hold values from 0 to 1023
- foot_wgt: float32 [256, 16], P('space'), may hold values from 0.05 to 0.2
- obs_value: float32 [256, 256], P('space'), may hold values from -6 to 6
- obs_rinv: float32 [256, 16], P('space'), may hold values from 0.5 to 4
- owner_counts: int32 [8, 8], P('space'), may hold values from 0 to 4, as said below
Outputs:
- gradient: bfloat16 [8192, 1536], P('space', 'var')
The draws below stay inside these ranges and needn't reach their ends.
Inputs may be any that keep to these rules, and one draw needn't show every extreme that they name: `neighbours`: neighbour 0 of each block is the block itself; every neighbour lies within 8 blocks of it, and on every tile some block has a neighbour exactly 8 blocks away. `owner_counts`: in every draw one owner receives 4 footprints from every tile.
All inputs are finite; a program needn't handle non-finite values.
Results may differ from the reference program's by a relative error of at most 0.0034.
Values may be sent and summed in bfloat16 or wider, within the bound.
No kernel may reach another device: no remote copies, remote signals or barrier semaphores. Data moves between devices by JAX's collectives and lax.ppermute only.
A program may use at most 64 MiB of HBM per device.

```python
import math
import jax
import jax.numpy as jnp
from jax import lax

NV = 96
BSZ = 128
K = 5
CH = 16
P_SIZE = 16
CAP = 4
M = 16
BLK_DEV = 8
TILES = 8
BLOCKS = 64
COLS_DEV = 1024
COLUMNS = 8192
SLOTS = 256


def draw_neighbours(key, part):
    key = jax.random.fold_in(key, 11)
    key_offs, key_pick = jax.random.split(key)
    rows = jnp.arange(BLOCKS, dtype=jnp.int32)
    offsets = jax.random.randint(key_offs, (BLOCKS, K), -BLK_DEV, BLK_DEV + 1)
    offsets = offsets.at[:, 0].set(0)
    tile_count = BLOCKS // BLK_DEV
    chosen_rows = jax.random.randint(key_pick, (tile_count,), 0, BLK_DEV)
    tile_of = rows // BLK_DEV
    chosen = rows % BLK_DEV == chosen_rows[tile_of]
    far_step = jnp.where(tile_of == tile_count - 1, -BLK_DEV, BLK_DEV)
    offsets = offsets.at[:, 1].set(jnp.where(chosen, far_step, offsets[:, 1]))
    return jnp.clip(rows[:, None] + offsets, 0, BLOCKS - 1).astype(jnp.int32)


def draw_owner_counts(key, part):
    key = jax.random.fold_in(key, 12)
    key_base, key_full = jax.random.split(key)
    base_counts = jax.random.randint(key_base, (TILES, TILES), 0, CAP + 1)
    full_owner = jax.random.randint(key_full, (), 0, TILES)
    owners = jnp.arange(TILES, dtype=jnp.int32)[None, :]
    return jnp.where(owners == full_owner, CAP, base_counts).astype(jnp.int32)


def touch_ends(entries, own_key, least, largest):
    dims = entries.shape
    place = [jax.random.randint(jax.random.fold_in(own_key, axis), (), 0, dims[axis]) for axis in range(len(dims))]
    entries = entries.at[tuple(place)].set(least)
    longest = dims.index(max(dims))
    place[longest] = (place[longest] + 1) % dims[longest]
    return entries.at[tuple(place)].set(largest)


def level_of(key, extent, pieces, smallest, largest):
    factor_of, own = 1.0, jax.random.fold_in(key, 6)
    for position, blocks in pieces:
        steps = jnp.exp(jax.random.uniform(jax.random.fold_in(own, position), (blocks,), jnp.float32, smallest / len(pieces), largest / len(pieces)))
        factor_of = factor_of * jnp.repeat(steps, extent[position] // blocks).reshape([-1 if axis == position else 1 for axis in range(len(extent))])
    return factor_of


def normal_values(rng, extent, spread, most, shards=(), kind=jnp.bfloat16):
    factor_of = level_of(rng, extent, shards, -0.22, 0.18) if shards else 1.0
    drawn = jax.random.normal(rng, extent, jnp.float32) * spread * factor_of
    return jnp.minimum(jnp.maximum(drawn, -most), most).astype(kind)


def setup_inputs(seed: int = 0) -> dict:
    key_of = jax.random.split(jax.random.key(seed), 11)
    control = normal_values(key_of[0], (COLUMNS, NV * M), 1.0, 6.0, ((0, 8), (1, 4)))
    roots = normal_values(key_of[1], (BLOCKS, K, BSZ, BSZ), (BSZ * K) ** -0.5, 0.25, ((0, 8),))
    neighbours = draw_neighbours(jax.random.fold_in(key_of[10], 71), 0)
    sigma = jnp.clip(jnp.exp(math.log(3.0) - 2.3025851 * jax.random.uniform(key_of[3], (NV, COLUMNS), jnp.float32) ** level_of(key_of[3], (NV, COLUMNS), ((0, 4), (1, 8)), -0.2, 0.2)), 0.3, 3.0)
    obs_op = normal_values(key_of[4], (NV, CH), NV ** -0.5, 0.625, ((0, 4),))
    foot_cols = touch_ends(jax.random.randint(key_of[5], (SLOTS, P_SIZE), 0, COLS_DEV), jax.random.fold_in(key_of[5], 1), 0, COLS_DEV - 1).astype(jnp.int32)
    foot_wgt = jnp.clip(0.05 + 0.15 * jax.random.uniform(key_of[6], (SLOTS, P_SIZE), jnp.float32) ** level_of(key_of[6], (SLOTS, P_SIZE), ((0, 8),), -0.2, 0.2), 0.05, 0.2)
    obs_value = normal_values(key_of[7], (SLOTS, CH * M), 1.0, 6.0, ((0, 8),), jnp.float32)
    obs_rinv = jnp.clip(jnp.exp(math.log(4.0) - 2.0794415 * jax.random.uniform(key_of[8], (SLOTS, CH), jnp.float32) ** level_of(key_of[8], (SLOTS, CH), ((0, 8),), -0.2, 0.2)), 0.5, 4.0)
    owner_counts = draw_owner_counts(jax.random.fold_in(key_of[10], 71), 0)
    return {"control": control, "roots": roots, "neighbours": neighbours, "sigma": sigma, "obs_op": obs_op, "foot_cols": foot_cols, "foot_wgt": foot_wgt, "obs_value": obs_value, "obs_rinv": obs_rinv, "owner_counts": owner_counts}


def round_part(values):
    narrow = lax.optimization_barrier(values.astype(jnp.bfloat16))
    return narrow.astype(jnp.float32)


def reference(control, roots, neighbours, sigma, obs_op, foot_cols, foot_wgt, obs_value, obs_rinv, owner_counts):
    groups = 4
    var_group = NV // groups
    group_width = var_group * M
    roots_f = roots.astype(jnp.float32)
    band_cols = jnp.zeros((COLUMNS, CH, M), jnp.float32)
    for group in range(groups):
        lo_col = group * group_width
        piece = control[:, lo_col:lo_col + group_width].reshape(BLOCKS, BSZ, group_width)
        summed = jnp.zeros((BLOCKS, BSZ, group_width), jnp.float32)
        for link_index in range(K):
            picked = jnp.take(piece, neighbours[:, link_index], axis=0).astype(jnp.float32)
            summed = summed + jnp.einsum('bij,bjn->bin', roots_f[:, link_index], picked)
        sig_rep = jnp.repeat(sigma[group * var_group:(group + 1) * var_group].T, M, axis=1)
        state_bf = (summed.reshape(COLUMNS, group_width) * sig_rep).astype(jnp.bfloat16)
        band_cols = band_cols + jnp.einsum('cjm,jh->chm', state_bf.reshape(COLUMNS, var_group, M).astype(jnp.float32), obs_op[group * var_group:(group + 1) * var_group].astype(jnp.float32))
    rows = jnp.arange(SLOTS, dtype=jnp.int32)
    global_cols = foot_cols + (rows // (TILES * CAP))[:, None] * COLS_DEV
    picked_bands = jnp.take(band_cols, global_cols, axis=0)
    modelled = jnp.sum(foot_wgt[:, :, None, None] * picked_bands, axis=1).reshape(SLOTS, CH * M)
    owner_order = modelled.reshape(TILES, TILES, CAP, CH * M).transpose(1, 0, 2, 3).reshape(SLOTS, CH * M)
    misfit_own = jnp.repeat(obs_rinv, M, axis=1) * (owner_order - obs_value)
    misfit = misfit_own.reshape(TILES, TILES, CAP, CH * M).transpose(1, 0, 2, 3).reshape(SLOTS, CH * M)
    live_mask = (jnp.arange(CAP)[None, None, :] < owner_counts[:, :, None]).reshape(SLOTS)
    misfit = jnp.where(live_mask[:, None], misfit, 0.0)
    spread_terms = foot_wgt[:, :, None] * misfit[:, None, :]
    pulled = jnp.zeros((COLUMNS, CH * M), jnp.float32).at[global_cols.reshape(-1)].add(spread_terms.reshape(-1, CH * M))
    pulled = pulled.reshape(COLUMNS, CH, M)
    source_tile = (jnp.arange(BLOCKS, dtype=jnp.int32) // BLK_DEV).astype(jnp.int32)
    outputs = []
    for group in range(groups):
        lo_col = group * group_width
        op_group = obs_op[group * var_group:(group + 1) * var_group].astype(jnp.float32)
        before = jnp.einsum('chm,jh->cjm', pulled, op_group, precision=lax.Precision.HIGHEST).reshape(COLUMNS, group_width)
        sig_rep = jnp.repeat(sigma[group * var_group:(group + 1) * var_group].T, M, axis=1)
        adjoint_in = (before * sig_rep).astype(jnp.bfloat16).reshape(BLOCKS, BSZ, group_width).astype(jnp.float32)
        own_part = jnp.zeros((BLOCKS, BSZ, group_width), jnp.float32)
        below_part = jnp.zeros((BLOCKS, BSZ, group_width), jnp.float32)
        above_part = jnp.zeros((BLOCKS, BSZ, group_width), jnp.float32)
        for link_index in range(K):
            terms = jnp.einsum('bji,bjn->bin', roots_f[:, link_index], adjoint_in)
            targets = neighbours[:, link_index]
            target_tile = (targets // BLK_DEV).astype(jnp.int32)
            same = (target_tile == source_tile)[:, None, None]
            from_below = (target_tile == source_tile + 1)[:, None, None]
            from_above = (target_tile + 1 == source_tile)[:, None, None]
            own_part = own_part.at[targets].add(jnp.where(same, terms, 0.0))
            below_part = below_part.at[targets].add(jnp.where(from_below, terms, 0.0))
            above_part = above_part.at[targets].add(jnp.where(from_above, terms, 0.0))
        adjoint_sum = own_part + round_part(below_part) + round_part(above_part)
        result = control[:, lo_col:lo_col + group_width].astype(jnp.float32) + adjoint_sum.reshape(COLUMNS, group_width)
        outputs.append(result.astype(jnp.bfloat16))
    return jnp.concatenate(outputs, axis=1)
```

```python
import functools

import jax
import jax.numpy as jnp
from jax import lax
from jax.experimental import pallas as pl
from jax.experimental.pallas import tpu as pltpu
from jax.sharding import PartitionSpec as P

F32 = jnp.float32
BF16 = jnp.bfloat16
LANES = 128
NT = (((1,), (1,)), ((), ()))


def repeat_steps(count, body):
    if count <= 2:
        for step in range(count):
            body(step)
    else:
        lax.fori_loop(0, count, lambda step, carry: (body(step), carry)[1], 0)


def at(step, size):
    if isinstance(step, int):
        return pl.ds(step * size, size)
    return pl.ds(pl.multiple_of(step * size, size), size)


def dot(a, b):
    return jnp.dot(a, b, preferred_element_type=F32)


def dot_nt(a, b):
    return lax.dot_general(a, b, NT, preferred_element_type=F32)


def split2(x):
    high = x.astype(BF16)
    return high, (x - high.astype(F32)).astype(BF16)


def iota(shape, axis):
    return lax.broadcasted_iota(jnp.int32, shape, axis)


def column(values):
    slots, width = values.shape
    wide = jnp.broadcast_to(values.astype(F32)[:, None, :], (slots, width, width))
    wide = wide.reshape(slots * width, width)
    hit = iota(wide.shape, 1) == lax.rem(iota(wide.shape, 0), width)
    return jnp.sum(jnp.where(hit, wide, 0.0), axis=1, keepdims=True)


def one_hot(cols, count):
    lane = iota((cols.shape[0], count), 1)
    return jnp.where(lane == cols.astype(jnp.int32), 1.0, 0.0).astype(BF16)


def scale_spread(dims, half):
    row = iota((LANES, dims.lanes), 0) - 2 * dims.vars * half
    lane = iota((LANES, dims.lanes), 1)
    first = lane - dims.members * row
    second = first + dims.members * dims.vars
    hit = ((first >= 0) & (first < dims.members)) | ((second >= 0) & (second < dims.members))
    return jnp.where(hit, 1.0, 0.0).astype(BF16)


def target_spread(dims, half):
    shape = (LANES, dims.others * dims.block)
    row = iota(shape, 0) - 4 * dims.vars - dims.others * half
    first = iota(shape, 1) - dims.block * row
    return jnp.where((first >= 0) & (first < dims.block), 1.0, 0.0).astype(BF16)


def fill_operator(dims, op_ref, targets, parts, shift):
    for q in range(dims.blocks):
        total = None
        for target, part in zip(targets, parts):
            term = jnp.where(target == float(q + shift), part, 0.0)
            total = term if total is None else total + term
        op_ref[:, q * dims.block : (q + 1) * dims.block] = total.astype(BF16)


def model_rows(dims, op_ref, plane, spread, control_ref, opw_ref):
    summed = dot(op_ref[...], control_ref[...])
    state = (summed * dot(plane, spread)).astype(BF16)
    bands = dot(state, opw_ref[...])
    return jnp.sum(bands.reshape(dims.chunk_slots, dims.points, bands.shape[1]), axis=1)


def select_kernel(dims, roots_ref, sigma_ref, cols_ref, wgt_ref, nb_ref, out_ref):
    tile = lax.axis_index("space")
    half = lax.rem(lax.axis_index("var"), 2)
    sigma = sigma_ref[...]
    rest = jnp.zeros((LANES - 2 * dims.vars, dims.columns), F32)
    sigma0 = split2(jnp.concatenate([sigma, sigma, rest], axis=0))
    pad = jnp.zeros((2 * dims.vars, dims.columns), F32)
    tail = jnp.zeros((LANES - 4 * dims.vars, dims.columns), F32)
    sigma1 = split2(jnp.concatenate([pad, sigma, sigma, tail], axis=0))
    nb = (nb_ref[...] - tile * dims.blocks).astype(F32)
    lane = iota((dims.blocks, LANES), 1)
    nbs = []
    for h in range(2):
        wide = jnp.zeros((dims.blocks, LANES), F32)
        for k in range(dims.others):
            wide = jnp.where(
                lane == 4 * dims.vars + dims.others * h + k, nb[:, k + 1 : k + 2], wide
            )
        nbs.append(wide.astype(BF16))

    def body(step):
        plane = jnp.zeros((dims.chunk, LANES), F32)
        for h, sigmas in ((0, sigma0), (1, sigma1)):
            slots = at(step + h * dims.half_chunks, dims.chunk_slots)
            cols = column(cols_ref[slots, :])
            hot = one_hot(cols, dims.columns)
            scale = dot_nt(hot, sigmas[0]) + dot_nt(hot, sigmas[1])
            hot_block = one_hot(jnp.floor(cols * (1.0 / dims.block)), dims.blocks)
            plane = plane + scale * column(wgt_ref[slots, :]) + dot(hot_block, nbs[h])
        lanes = iota((dims.chunk, LANES), 1)
        low = ((lanes >= dims.vars) & (lanes < 2 * dims.vars)) | (
            (lanes >= 3 * dims.vars) & (lanes < 4 * dims.vars)
        )
        high = plane.astype(BF16).astype(F32)
        rows = at(step, dims.chunk)
        wide = dims.others * dims.block
        out_ref[rows, wide : wide + LANES] = jnp.where(low, plane - high, high).astype(BF16)
        slots = at(step + half * dims.half_chunks, dims.chunk_slots)
        hot = one_hot(column(cols_ref[slots, :]), dims.columns)
        for k in range(dims.others):
            root = roots_ref[:, k + 1].reshape(dims.columns, dims.block)
            out_ref[rows, k * dims.block : (k + 1) * dims.block] = dot(hot, root).astype(BF16)

    repeat_steps(dims.half_chunks, body)


def own_kernel(
    dims, roots_ref, cols_ref, plane_ref, control_ref, opw_ref, model_ref, opt_ref, op_ref
):
    for h in range(2):
        spread = scale_spread(dims, h)
        targets_of = target_spread(dims, h)

        def body(step):
            plane = plane_ref[at(step, dims.chunk), :]
            slots = at(step + h * dims.half_chunks, dims.chunk_slots)
            cols = column(cols_ref[slots, :])
            hot = one_hot(cols, dims.columns)
            wide = dot(plane, targets_of)
            own = jnp.broadcast_to(
                jnp.floor(cols * (1.0 / dims.block)), (dims.chunk, dims.block)
            )
            targets, parts = [own], []
            for k in range(dims.others):
                targets.append(wide[:, k * dims.block : (k + 1) * dims.block])
            for k in range(dims.others + 1):
                root = roots_ref[:, k].reshape(dims.columns, dims.block)
                parts.append(dot(hot, root))
            fill_operator(dims, op_ref, targets, parts, 0)
            model_ref[slots, :] = model_rows(dims, op_ref, plane, spread, control_ref, opw_ref)
            opt_ref[:, at(step + h * dims.half_chunks, dims.chunk)] = op_ref[...].T

        repeat_steps(dims.half_chunks, body)


def side_parts(dims, plane_ref, message_ref, step, targets_of):
    rows = at(step, dims.chunk)
    wide = dims.others * dims.block
    plane = plane_ref[rows, wide : wide + LANES]
    target = dot(plane, targets_of)
    targets, parts = [], []
    for k in range(dims.others):
        lanes = slice(k * dims.block, (k + 1) * dims.block)
        targets.append(target[:, lanes])
        parts.append(message_ref[rows, lanes].astype(F32))
    return plane, targets, parts


def sides_kernel(dims, b0_ref, b1_ref, a0_ref, a1_ref, control_ref, opw_ref, below_ref, above_ref, op_ref):
    half = lax.rem(lax.axis_index("var"), 2)
    for which, refs in ((half, (b0_ref, a0_ref)), (1 - half, (b1_ref, a1_ref))):
        spread = scale_spread(dims, which)
        targets_of = target_spread(dims, which)
        for side, (ref, model_ref) in enumerate(zip(refs, (below_ref, above_ref))):
            plane_ref = (b0_ref, a0_ref)[side]
            shift = (dims.blocks, -dims.blocks)[side]

            def body(step):
                plane, targets, parts = side_parts(dims, plane_ref, ref, step, targets_of)
                fill_operator(dims, op_ref, targets, parts, shift)
                slots = at(step + which * dims.half_chunks, dims.chunk_slots)
                model_ref[slots, :] = model_rows(
                    dims, op_ref, plane, spread, control_ref, opw_ref
                )

            repeat_steps(dims.half_chunks, body)


def turn_kernel(dims, b0_ref, b1_ref, a0_ref, a1_ref, opt_ref, op_ref):
    half = lax.rem(lax.axis_index("var"), 2)
    for place, (which, refs) in enumerate(
        ((half, (b0_ref, a0_ref)), (1 - half, (b1_ref, a1_ref)))
    ):
        targets_of = target_spread(dims, which)
        for side, (ref, shift) in enumerate(zip(refs, (dims.blocks, -dims.blocks))):
            plane_ref = (b0_ref, a0_ref)[side]

            def body(step):
                _, targets, parts = side_parts(dims, plane_ref, ref, step, targets_of)
                fill_operator(dims, op_ref, targets, parts, shift)
                chunk = step + (2 * side + place) * dims.half_chunks
                opt_ref[:, at(chunk, dims.chunk)] = op_ref[...].T

            repeat_steps(dims.half_chunks, body)


def pull_rows(dims, w_ref, slots, scale):
    rows = w_ref[slots, :]
    wide = jnp.broadcast_to(
        rows[:, None, :], (dims.chunk_slots, dims.points, dims.lanes)
    ).reshape(dims.chunk, dims.lanes)
    return (wide * scale).astype(BF16)


def bands_to_vars(misfit, opw):
    high = misfit.astype(BF16)
    rest = misfit - high.astype(F32)
    middle = rest.astype(BF16)
    low = (rest - middle.astype(F32)).astype(BF16)
    return dot_nt(high, opw) + (dot_nt(middle, opw) + dot_nt(low, opw))


def own_adjoint_kernel(dims, misfit_ref, plane_ref, opt_ref, control_ref, opw_ref, out_ref, w_ref, adj_ref):
    w_ref[...] = bands_to_vars(misfit_ref[...], opw_ref[...])
    for h in range(2):
        spread = scale_spread(dims, h)

        def body(step):
            scale = dot(plane_ref[at(step, dims.chunk), :], spread)
            chunk = step + h * dims.half_chunks
            adj_ref[at(chunk, dims.chunk), :] = pull_rows(
                dims, w_ref, at(chunk, dims.chunk_slots), scale
            )

        repeat_steps(dims.half_chunks, body)
    for part in range(dims.columns // 256):
        rows = slice(part * 256, (part + 1) * 256)
        out_ref[rows, :] = control_ref[rows, :].astype(F32) + dot(opt_ref[rows, :], adj_ref[...])


def sides_adjoint_kernel(
    dims, mb_ref, ma_ref, below_ref, above_ref, opt_ref, own_ref, opw_ref, out_ref, w_ref, adj_ref
):
    half = lax.rem(lax.axis_index("var"), 2)
    spreads = [scale_spread(dims, half), scale_spread(dims, 1 - half)]
    for side, (misfit_ref, ref) in enumerate(((mb_ref, below_ref), (ma_ref, above_ref))):
        w_ref[...] = bands_to_vars(misfit_ref[...], opw_ref[...])
        for place, which in enumerate((half, 1 - half)):

            def body(step):
                scale = dot(ref[at(step, dims.chunk), :], spreads[place])
                chunk = step + (2 * side + place) * dims.half_chunks
                slots = at(step + which * dims.half_chunks, dims.chunk_slots)
                adj_ref[at(chunk, dims.chunk), :] = pull_rows(dims, w_ref, slots, scale)

            repeat_steps(dims.half_chunks, body)
    for part in range(dims.columns // 256):
        rows = slice(part * 256, (part + 1) * 256)
        total = own_ref[rows, :] + dot(opt_ref[rows, :], adj_ref[...])
        out_ref[rows, :] = total.astype(BF16)


class Dims:
    def __init__(self, control, roots, sigma, foot_cols):
        self.blocks, links, self.block = roots.shape[:3]
        self.others = links - 1
        self.columns, self.lanes = control.shape
        self.vars = sigma.shape[0]
        self.members = self.lanes // self.vars
        self.slots, self.points = foot_cols.shape
        self.rows = self.slots * self.points
        self.chunk = min(256, self.rows // 2)
        self.chunk_slots = self.chunk // self.points
        self.half_chunks = self.rows // 2 // self.chunk
        self.width = self.others * self.block + LANES


def call(kernel, name, out_shape, scratch, flops, in_specs=None):
    specs = {} if in_specs is None else {"in_specs": in_specs, "grid": (1,)}
    if in_specs is not None:
        specs["out_specs"] = jax.tree.map(
            lambda s: pl.BlockSpec(s.shape, lambda i, n=len(s.shape): (0,) * n), out_shape
        )
    return pl.pallas_call(
        kernel,
        out_shape=out_shape,
        scratch_shapes=scratch,
        compiler_params=pltpu.CompilerParams(vmem_limit_bytes=56 * 1024 * 1024),
        cost_estimate=pl.CostEstimate(flops=flops, bytes_accessed=4000000, transcendentals=0),
        name=name,
        **specs,
    )


def whole(array):
    return pl.BlockSpec(array.shape, lambda i, n=array.ndim: (0,) * n)


def shards(
    control,
    roots,
    neighbours,
    sigma,
    obs_op,
    foot_cols,
    foot_wgt,
    obs_value,
    obs_rinv,
    owner_counts,
):
    dims = Dims(control, roots, sigma, foot_cols)
    bands = obs_op.shape[1]
    members = dims.members
    tiles = lax.axis_size("space")
    ranks = lax.axis_size("var")
    forward = [(i, i + 1) for i in range(tiles - 1)]
    backward = [(i + 1, i) for i in range(tiles - 1)]
    up = lambda x: lax.ppermute(x, "space", forward)
    down = lambda x: lax.ppermute(x, "space", backward)
    swap = lambda x, bit: lax.ppermute(x, "var", [(i, i ^ bit) for i in range(ranks)])
    shape = jax.ShapeDtypeStruct
    half_rows = dims.rows // 2
    flat = bands * members

    message = call(
        functools.partial(select_kernel, dims),
        "select",
        shape((half_rows, dims.width), BF16),
        [],
        2000000000,
    )(roots, sigma, foot_cols, foot_wgt, neighbours)
    below0, above0 = up(message), down(message)
    below1, above1 = swap(below0, 1), swap(above0, 1)

    identity_m = jnp.eye(members, dtype=BF16)
    opw = (obs_op[:, None, :, None] * identity_m[None, :, None, :]).reshape(dims.lanes, flat)
    observed = lax.all_to_all(
        jnp.concatenate([obs_value, obs_rinv], axis=1), "space", 0, 0, tiled=True
    )
    capacity = dims.slots // owner_counts.shape[1]
    slot_ids = jnp.arange(dims.slots, dtype=jnp.int32)
    live = slot_ids % capacity < jnp.repeat(owner_counts[0], capacity)
    rinv = jnp.repeat(jnp.where(live[:, None], observed[:, flat:], 0.0), members, axis=1)
    value = observed[:, :flat]

    plane_spec = pl.BlockSpec((half_rows, LANES), lambda i: (0, dims.others * dims.block // LANES))
    own_model, own_opt = call(
        functools.partial(own_kernel, dims),
        "own_model",
        (shape((dims.slots, flat), F32), shape((dims.columns, dims.rows), BF16)),
        [pltpu.VMEM((dims.chunk, dims.columns), BF16)],
        4000000000,
        [whole(roots), whole(foot_cols), plane_spec, whole(control), whole(opw)],
    )(roots, foot_cols, message, control, opw)

    sides = (below0, below1, above0, above1)
    part_below, part_above = call(
        functools.partial(sides_kernel, dims),
        "sides_model",
        (shape((dims.slots, flat), F32),) * 2,
        [pltpu.VMEM((dims.chunk, dims.columns), BF16)],
        4000000000,
    )(*sides, control, opw)
    modelled = own_model + down(part_below) + up(part_above)
    bit = 1
    while bit < ranks:
        modelled = modelled + swap(modelled, bit)
        bit *= 2
    misfit = rinv * (modelled - value)
    misfit_below, misfit_above = up(misfit), down(misfit)

    sides_opt = call(
        functools.partial(turn_kernel, dims),
        "sides_turn",
        shape((dims.columns, 2 * dims.rows), BF16),
        [pltpu.VMEM((dims.chunk, dims.columns), BF16)],
        4000000000,
    )(*sides)
    own_total = call(
        functools.partial(own_adjoint_kernel, dims),
        "own_adjoint",
        shape((dims.columns, dims.lanes), F32),
        [pltpu.VMEM((dims.slots, dims.lanes), F32), pltpu.VMEM((dims.rows, dims.lanes), BF16)],
        2000000000,
        [whole(misfit), plane_spec, whole(own_opt), whole(control), whole(opw)],
    )(misfit, message, own_opt, control, opw)
    return call(
        functools.partial(sides_adjoint_kernel, dims),
        "sides_adjoint",
        shape((dims.columns, dims.lanes), BF16),
        [pltpu.VMEM((dims.slots, dims.lanes), F32), pltpu.VMEM((2 * dims.rows, dims.lanes), BF16)],
        4000000000,
        [whole(misfit), whole(misfit)] + [plane_spec] * 2 + [whole(sides_opt), whole(own_total), whole(opw)],
    )(misfit_below, misfit_above, below0, above0, sides_opt, own_total, opw)


def solution(mesh):
    return jax.shard_map(
        shards,
        mesh=mesh,
        in_specs=(
            P("space", "var"),
            P("space", None, None, None),
            P("space", None),
            P("var", "space"),
            P("var", None),
            P("space", None),
            P("space", None),
            P("space", None),
            P("space", None),
            P("space", None),
        ),
        out_specs=P("space", "var"),
        check_vma=False,
    )
```

```python
import functools

import jax
import jax.numpy as jnp
from jax import lax
from jax.experimental import pallas as pl
from jax.experimental.pallas import tpu as pltpu
from jax.sharding import PartitionSpec as P

F32 = jnp.float32
BF16 = jnp.bfloat16
LANES = 128
NT = (((1,), (1,)), ((), ()))


def repeat_steps(count, body):
    if count <= 2:
        for step in range(count):
            body(step)
    else:
        lax.fori_loop(0, count, lambda step, carry: (body(step), carry)[1], 0)


def at(step, size):
    if isinstance(step, int):
        return pl.ds(step * size, size)
    return pl.ds(pl.multiple_of(step * size, size), size)


def dot(a, b):
    return jnp.dot(a, b, preferred_element_type=F32)


def dot_nt(a, b):
    return lax.dot_general(a, b, NT, preferred_element_type=F32)


def iota(shape, axis):
    return lax.broadcasted_iota(jnp.int32, shape, axis)


def column(values):
    points, slots = values.shape
    wide = jnp.broadcast_to(values.astype(F32)[:, None, :], (points, slots, slots))
    wide = wide.reshape(points * slots, slots)
    hit = iota(wide.shape, 1) == lax.rem(iota(wide.shape, 0), slots)
    return jnp.sum(jnp.where(hit, wide, 0.0), axis=1, keepdims=True)


def one_hot(cols, count):
    lane = iota((cols.shape[0], count), 1)
    return jnp.where(lane == cols.astype(jnp.int32), 1.0, 0.0).astype(BF16)


def within(value, low, count):
    return (value >= low) & (value < low + count)


def as_bf16(mask):
    return jnp.where(mask, 1.0, 0.0).astype(BF16)


def scale_spread(dims, half):
    shape = (LANES, dims.lanes)
    first = iota(shape, 1) - dims.members * (iota(shape, 0) - dims.vars * half)
    second = first + dims.members * 2 * dims.vars
    return as_bf16(within(first, 0, dims.members) | within(second, 0, dims.members))


def target_spread(dims):
    shape = (LANES, dims.others * dims.block)
    return as_bf16(
        within(iota(shape, 1) - dims.block * (iota(shape, 0) - 4 * dims.vars), 0, dims.block)
    )


def fill_operator(dims, op_ref, targets, parts):
    for q in range(dims.blocks):
        total = None
        for target, part in zip(targets, parts):
            term = jnp.where(target == jnp.asarray(q, target.dtype), part, jnp.zeros((), part.dtype))
            total = term if total is None else total + term
        op_ref[:, q * dims.block : (q + 1) * dims.block] = total


def model_rows(dims, op_ref, plane, spread, control_ref, opw):
    summed = dot(op_ref[...], control_ref[...])
    state = (summed * dot(plane, spread)).astype(BF16)
    bands = dot(state, opw)
    return jnp.sum(bands.reshape(dims.chunk_points, dims.slots, bands.shape[1]), axis=0)


def select_kernel(dims, roots_ref, sigma_ref, sigma2_ref, cols_ref, wgt_ref, nb_ref, out_ref):
    tile = lax.axis_index("space")
    half = lax.rem(lax.axis_index("var"), 2)
    sigma, sigma2 = sigma_ref[...], sigma2_ref[...]
    sigma = jnp.concatenate(
        [jnp.where(half == 0, sigma, sigma2), jnp.where(half == 0, sigma2, sigma)], axis=0
    )
    high = sigma.astype(BF16).astype(F32)
    nb = nb_ref[...] + ((2 * half - 1) - tile) * dims.blocks
    nb = nb.astype(F32)
    base = 4 * dims.vars
    ids = jnp.zeros((LANES - base, dims.columns), F32)
    shape = ids.shape
    for b in range(dims.blocks):
        in_block = within(iota(shape, 1), b * dims.block, dims.block)
        for k in range(dims.others):
            ids = jnp.where(in_block & (iota(shape, 0) == k), nb[b : b + 1, k + 1 : k + 2], ids)
    table = jnp.concatenate([high, sigma - high, ids], axis=0).astype(BF16)
    row, lane = iota((LANES, LANES), 0), iota((LANES, LANES), 1)
    fold = as_bf16(
        (row == lane)
        | ((row < base) & (lane < base) & ((row == lane + base // 2) | (lane == row + base // 2)))
    )
    wide = dims.others * dims.block

    def body(step):
        points = at(step, dims.chunk_points)
        hot = one_hot(column(cols_ref[points, :]), dims.columns)
        plane = dot(dot_nt(hot, table).astype(BF16), fold)
        lanes = iota((dims.chunk, LANES), 1)
        plane = jnp.where(lanes < base, plane * column(wgt_ref[points, :]), plane)
        top = plane.astype(BF16).astype(F32)
        rows = at(step, dims.chunk)
        out_ref[rows, wide:] = jnp.where(
            within(lanes, base // 2, base // 2), plane - top, top
        ).astype(BF16)
        for k in range(0, dims.others, 2):
            pair = range(k, min(k + 2, dims.others))
            root = jnp.concatenate(
                [roots_ref[:, i + 1].reshape(dims.columns, dims.block) for i in pair], axis=1
            )
            out_ref[rows, k * dims.block : (k + len(pair)) * dims.block] = dot(hot, root).astype(BF16)

    repeat_steps(dims.chunks, body)


def own_kernel(
    dims, roots_ref, cols_ref, message_ref, control_ref, obs_ref,
    model_ref, opt_ref, opw_ref, op_ref,
):
    half = lax.rem(lax.axis_index("var"), 2)
    bands = obs_ref.shape[0]
    flat = bands * dims.members
    vars_wide = as_bf16(
        within(iota((dims.lanes, dims.vars), 0) - dims.members * iota((dims.lanes, dims.vars), 1), 0, dims.members)
    )
    bands_wide = as_bf16(
        within(iota((bands, flat), 1) - dims.members * iota((bands, flat), 0), 0, dims.members)
    )
    opw = dot(dot_nt(vars_wide, obs_ref[...]).astype(BF16), bands_wide)
    same = lax.rem(iota(opw.shape, 0), dims.members) == lax.rem(iota(opw.shape, 1), dims.members)
    opw = jnp.where(same, opw, 0.0).astype(BF16)
    opw_ref[...] = opw
    spread, targets_of = scale_spread(dims, half), target_spread(dims)
    root = roots_ref[:, 0].reshape(dims.columns, dims.block)
    shift = ((1 - 2 * half) * dims.blocks).astype(F32)

    def body(step):
        rows = at(step, dims.chunk)
        wide = dims.others * dims.block
        plane = message_ref[rows, wide:]
        cols = column(cols_ref[at(step, dims.chunk_points), :])
        own = jnp.floor(cols * (1.0 / dims.block))
        targets = [jnp.broadcast_to(own, (dims.chunk, dims.block)).astype(BF16)]
        parts = [dot(one_hot(cols, dims.columns), root).astype(BF16)]
        ids = (dot(plane, targets_of) + shift).astype(BF16)
        for k in range(dims.others):
            lanes = slice(k * dims.block, (k + 1) * dims.block)
            targets.append(ids[:, lanes])
            parts.append(message_ref[rows, lanes])
        fill_operator(dims, op_ref, targets, parts)
        model = model_rows(dims, op_ref, plane, spread, control_ref, opw)
        if isinstance(step, int) and step == 0:
            model_ref[...] = model
        else:
            model_ref[...] += model
        opt_ref[:, rows] = op_ref[...].T

    if dims.chunks > 2:
        model_ref[...] = jnp.zeros_like(model_ref)
    repeat_steps(dims.chunks, body)


def side_parts(dims, message_ref, step, targets_of):
    rows = at(step, dims.chunk)
    wide = dims.others * dims.block
    plane = message_ref[rows, wide:]
    ids = dot(plane, targets_of).astype(BF16)
    lanes = [slice(k * dims.block, (k + 1) * dims.block) for k in range(dims.others)]
    return plane, [ids[:, l] for l in lanes], [message_ref[rows, l] for l in lanes]


def sides_kernel(dims, mine_ref, other_ref, own_ref, control_ref, opw_ref, keep_ref, give_ref, op_ref):
    half = lax.rem(lax.axis_index("var"), 2)
    spread, targets_of = scale_spread(dims, half), target_spread(dims)
    opw = opw_ref[...]
    give_ref[dims.slots :, :] = own_ref[...]
    for ref, model_ref in ((mine_ref, keep_ref), (other_ref, give_ref.at[: dims.slots])):

        def body(step):
            plane, targets, parts = side_parts(dims, ref, step, targets_of)
            fill_operator(dims, op_ref, targets, parts)
            model = model_rows(dims, op_ref, plane, spread, control_ref, opw)
            if isinstance(step, int) and step == 0:
                model_ref[...] = model
            else:
                model_ref[...] += model

        if dims.chunks > 2:
            model_ref[...] = jnp.zeros_like(model_ref)
        repeat_steps(dims.chunks, body)


def turn_kernel(dims, mine_ref, other_ref, opt_ref):
    targets_of = target_spread(dims)
    for side, ref in enumerate((mine_ref, other_ref)):

        def body(step):
            _, targets, parts = side_parts(dims, ref, step, targets_of)
            targets = [target.T for target in targets]
            parts = [part.T for part in parts]
            lanes = at(step + side * dims.chunks, dims.chunk)
            for q in range(dims.blocks):
                total = None
                for target, part in zip(targets, parts):
                    term = jnp.where(target == jnp.asarray(q, BF16), part, jnp.zeros((), BF16))
                    total = term if total is None else total + term
                opt_ref[q * dims.block : (q + 1) * dims.block, lanes] = total

        repeat_steps(dims.chunks, body)


def pull_rows(dims, pulled, scale):
    wide = scale.reshape(dims.chunk_points, dims.slots, dims.lanes) * pulled[None]
    return wide.reshape(dims.chunk, dims.lanes).astype(BF16)


def bands_to_vars(misfit, opw):
    high = misfit.astype(BF16)
    rest = misfit - high.astype(F32)
    middle = rest.astype(BF16)
    low = (rest - middle.astype(F32)).astype(BF16)
    return dot_nt(high, opw) + (dot_nt(middle, opw) + dot_nt(low, opw))


def own_adjoint_kernel(dims, misfit_ref, plane_ref, opt_ref, control_ref, opw_ref, out_ref, adj_ref):
    half = lax.rem(lax.axis_index("var"), 2)
    spread = scale_spread(dims, half)
    pulled = bands_to_vars(misfit_ref[...], opw_ref[...])

    def body(step):
        rows = at(step, dims.chunk)
        adj_ref[rows, :] = pull_rows(dims, pulled, dot(plane_ref[rows, :], spread))

    repeat_steps(dims.chunks, body)
    for part in range(dims.columns // 256):
        rows = slice(part * 256, (part + 1) * 256)
        out_ref[rows, :] = control_ref[rows, :].astype(F32) + dot(opt_ref[rows, :], adj_ref[...])


def sides_adjoint_kernel(
    dims, misfit_ref, misfit2_ref, mine_ref, other_ref, opt_ref, own_ref, opw_ref, out_ref, adj_ref
):
    half = lax.rem(lax.axis_index("var"), 2)
    spread = scale_spread(dims, half)
    for side, (values_ref, ref) in enumerate(((misfit_ref, mine_ref), (misfit2_ref, other_ref))):
        pulled = bands_to_vars(values_ref[...], opw_ref[...])

        def body(step):
            scale = dot(ref[at(step, dims.chunk), :], spread)
            adj_ref[at(step + side * dims.chunks, dims.chunk), :] = pull_rows(dims, pulled, scale)

        repeat_steps(dims.chunks, body)
    for part in range(dims.columns // 256):
        rows = slice(part * 256, (part + 1) * 256)
        total = own_ref[rows, :] + dot(opt_ref[rows, :], adj_ref[...])
        out_ref[rows, :] = total.astype(BF16)


class Dims:
    def __init__(self, control, roots, sigma, foot_cols):
        self.blocks, links, self.block = roots.shape[:3]
        self.others = links - 1
        self.columns, self.lanes = control.shape
        self.vars = sigma.shape[0]
        self.members = self.lanes // self.vars
        self.slots, self.points = foot_cols.shape
        self.rows = self.slots * self.points
        self.chunk_points = min(self.points, max(8, 512 // self.slots))
        self.chunk = self.chunk_points * self.slots
        self.chunks = self.rows // self.chunk
        self.width = self.others * self.block + LANES


def whole(array):
    return pl.BlockSpec(array.shape, lambda i, n=len(array.shape): (0,) * n)


def call(kernel, name, out_shape, scratch, flops, in_specs=None):
    specs = {}
    if in_specs is not None:
        specs = {"in_specs": in_specs, "grid": (1,), "out_specs": jax.tree.map(whole, out_shape)}
    return pl.pallas_call(
        kernel,
        out_shape=out_shape,
        scratch_shapes=scratch,
        compiler_params=pltpu.CompilerParams(vmem_limit_bytes=56 * 1024 * 1024),
        cost_estimate=pl.CostEstimate(flops=flops, bytes_accessed=4000000, transcendentals=0),
        name=name,
        **specs,
    )


def shards(
    control,
    roots,
    neighbours,
    sigma,
    obs_op,
    foot_cols,
    foot_wgt,
    obs_value,
    obs_rinv,
    owner_counts,
):
    dims = Dims(control, roots, sigma, foot_cols)
    bands = obs_op.shape[1]
    members = dims.members
    tiles = lax.axis_size("space")
    ranks = lax.axis_size("var")
    outward, inward = [], []
    for t in range(tiles):
        for v in range(ranks):
            to = t + 1 - 2 * (v % 2)
            if 0 <= to < tiles:
                outward.append((t * ranks + v, to * ranks + v))
                inward.append((to * ranks + v, t * ranks + v))
    hop = lambda x, pairs: lax.ppermute(x, ("space", "var"), pairs)
    swap = lambda x, bit: lax.ppermute(x, "var", [(i, i ^ bit) for i in range(ranks)])
    shape = jax.ShapeDtypeStruct
    flat = bands * members
    cols_t, wgt_t = foot_cols.T, foot_wgt.T

    message = call(
        functools.partial(select_kernel, dims),
        "select",
        shape((dims.rows, dims.width), BF16),
        [],
        2000000000,
    )(roots, sigma, swap(sigma, 1), cols_t, wgt_t, neighbours)
    mine = hop(message, outward)

    message, obs_value, obs_rinv = lax.optimization_barrier((message, obs_value, obs_rinv))
    observed = lax.all_to_all(
        jnp.concatenate([obs_value, obs_rinv], axis=1), "space", 0, 0, tiled=True
    )
    capacity = dims.slots // owner_counts.shape[1]
    slot_ids = jnp.arange(dims.slots, dtype=jnp.int32)
    live = slot_ids % capacity < jnp.repeat(owner_counts[0], capacity)
    rinv = jnp.repeat(jnp.where(live[:, None], observed[:, flat:], 0.0), members, axis=1)
    value = observed[:, :flat]

    own_model, own_opt, opw = call(
        functools.partial(own_kernel, dims),
        "own_model",
        (
            shape((dims.slots, flat), F32),
            shape((dims.columns, dims.rows), BF16),
            shape((dims.lanes, flat), BF16),
        ),
        [pltpu.VMEM((dims.chunk, dims.columns), BF16)],
        4000000000,
    )(roots, cols_t, message, control, obs_op.T)

    mine, own_model, own_opt, rinv, value = lax.optimization_barrier(
        (mine, own_model, own_opt, rinv, value)
    )
    other = swap(mine, 1)
    keep, give = call(
        functools.partial(sides_kernel, dims),
        "sides_model",
        (shape((dims.slots, flat), F32), shape((2 * dims.slots, flat), F32)),
        [pltpu.VMEM((dims.chunk, dims.columns), BF16)],
        4000000000,
    )(mine, other, own_model, control, opw)
    got = swap(give, 1)
    arrived = hop(keep + got[: dims.slots], inward)
    sides_opt = call(
        functools.partial(turn_kernel, dims),
        "sides_turn",
        shape((dims.columns, 2 * dims.rows), BF16),
        [],
        4000000000,
    )(mine, other)
    arrived, sides_opt = lax.optimization_barrier((arrived, sides_opt))
    modelled = own_model + got[dims.slots :] + arrived + swap(arrived, 1)
    bit = 2
    while bit < ranks:
        modelled = modelled + swap(modelled, bit)
        bit *= 2
    misfit = rinv * (modelled - value)
    misfit_mine = hop(misfit, outward)

    plane = pl.BlockSpec((dims.rows, LANES), lambda i: (0, dims.others * dims.block // LANES))
    own_total = call(
        functools.partial(own_adjoint_kernel, dims),
        "own_adjoint",
        shape((dims.columns, dims.lanes), F32),
        [pltpu.VMEM((dims.rows, dims.lanes), BF16)],
        2000000000,
        [whole(misfit), plane, whole(own_opt), whole(control), whole(opw)],
    )(misfit, message, own_opt, control, opw)
    misfit_mine, own_total = lax.optimization_barrier((misfit_mine, own_total))
    misfit_other = swap(misfit_mine, 1)
    return call(
        functools.partial(sides_adjoint_kernel, dims),
        "sides_adjoint",
        shape((dims.columns, dims.lanes), BF16),
        [pltpu.VMEM((2 * dims.rows, dims.lanes), BF16)],
        4000000000,
        [whole(misfit)] * 2 + [plane] * 2 + [whole(sides_opt), whole(own_total), whole(opw)],
    )(misfit_mine, misfit_other, mine, other, sides_opt, own_total, opw)


def solution(mesh):
    return jax.shard_map(
        shards,
        mesh=mesh,
        in_specs=(
            P("space", "var"),
            P("space", None, None, None),
            P("space", None),
            P("var", "space"),
            P("var", None),
            P("space", None),
            P("space", None),
            P("space", None),
            P("space", None),
            P("space", None),
        ),
        out_specs=P("space", "var"),
        check_vma=False,
    )
```

```python
import functools

import jax
import jax.numpy as jnp
from jax import lax
from jax.experimental import pallas as pl
from jax.experimental.pallas import tpu as pltpu
from jax.sharding import PartitionSpec as P

F32 = jnp.float32
BF16 = jnp.bfloat16
LANES = 128
NT = (((1,), (1,)), ((), ()))


def repeat_steps(count, body):
    if count <= 2:
        for step in range(count):
            body(step)
    else:
        lax.fori_loop(0, count, lambda step, carry: (body(step), carry)[1], 0)


def at(step, size):
    if isinstance(step, int):
        return pl.ds(step * size, size)
    return pl.ds(pl.multiple_of(step * size, size), size)


def dot(a, b):
    return jnp.dot(a, b, preferred_element_type=F32)


def dot_nt(a, b):
    return lax.dot_general(a, b, NT, preferred_element_type=F32)


def iota(shape, axis):
    return lax.broadcasted_iota(jnp.int32, shape, axis)


def column(values):
    points, slots = values.shape
    wide = jnp.broadcast_to(values.astype(F32)[:, None, :], (points, slots, slots))
    wide = wide.reshape(points * slots, slots)
    hit = iota(wide.shape, 1) == lax.rem(iota(wide.shape, 0), slots)
    return jnp.sum(jnp.where(hit, wide, 0.0), axis=1, keepdims=True)


def one_hot(cols, count):
    lane = iota((cols.shape[0], count), 1)
    return jnp.where(lane == cols.astype(jnp.int32), 1.0, 0.0).astype(BF16)


def within(value, low, count):
    return (value >= low) & (value < low + count)


def as_bf16(mask):
    return jnp.where(mask, 1.0, 0.0).astype(BF16)


def scale_spread(dims, half):
    shape = (LANES, dims.lanes)
    first = iota(shape, 1) - dims.members * (iota(shape, 0) - dims.vars * half)
    second = first + dims.members * 2 * dims.vars
    return as_bf16(within(first, 0, dims.members) | within(second, 0, dims.members))


def target_spread(dims):
    shape = (LANES, dims.others * dims.block)
    return as_bf16(
        within(iota(shape, 1) - dims.block * (iota(shape, 0) - 4 * dims.vars), 0, dims.block)
    )


def fill_operator(dims, op_ref, targets, parts):
    for q in range(dims.blocks):
        total = None
        for target, part in zip(targets, parts):
            term = jnp.where(target == jnp.asarray(q, target.dtype), part, jnp.zeros((), part.dtype))
            total = term if total is None else total + term
        op_ref[:, q * dims.block : (q + 1) * dims.block] = total


def model_rows(dims, op_ref, plane, spread, control_ref, opw):
    summed = dot(op_ref[...], control_ref[...])
    state = (summed * dot(plane, spread)).astype(BF16)
    bands = dot(state, opw)
    return jnp.sum(bands.reshape(dims.chunk_points, dims.slots, bands.shape[1]), axis=0)


def select_kernel(dims, roots_ref, sigma_ref, sigma2_ref, cols_ref, wgt_ref, nb_ref, out_ref):
    tile = lax.axis_index("space")
    half = lax.rem(lax.axis_index("var"), 2)
    sigma, sigma2 = sigma_ref[...], sigma2_ref[...]
    sigma = jnp.concatenate(
        [jnp.where(half == 0, sigma, sigma2), jnp.where(half == 0, sigma2, sigma)], axis=0
    )
    high = sigma.astype(BF16).astype(F32)
    nb = nb_ref[...] + ((2 * half - 1) - tile) * dims.blocks
    nb = nb.astype(F32)
    base = 4 * dims.vars
    ids = jnp.zeros((LANES - base, dims.columns), F32)
    shape = ids.shape
    for b in range(dims.blocks):
        in_block = within(iota(shape, 1), b * dims.block, dims.block)
        for k in range(dims.others):
            ids = jnp.where(in_block & (iota(shape, 0) == k), nb[b : b + 1, k + 1 : k + 2], ids)
    table = jnp.concatenate([high, sigma - high, ids], axis=0).astype(BF16)
    row, lane = iota((LANES, LANES), 0), iota((LANES, LANES), 1)
    fold = as_bf16(
        (row == lane)
        | ((row < base) & (lane < base) & ((row == lane + base // 2) | (lane == row + base // 2)))
    )
    wide = dims.others * dims.block

    def body(step):
        points = at(step, dims.chunk_points)
        hot = one_hot(column(cols_ref[points, :]), dims.columns)
        plane = dot(dot_nt(hot, table).astype(BF16), fold)
        lanes = iota((dims.chunk, LANES), 1)
        plane = jnp.where(lanes < base, plane * column(wgt_ref[points, :]), plane)
        top = plane.astype(BF16).astype(F32)
        rows = at(step, dims.chunk)
        out_ref[rows, wide:] = jnp.where(
            within(lanes, base // 2, base // 2), plane - top, top
        ).astype(BF16)
        for k in range(0, dims.others, 2):
            pair = range(k, min(k + 2, dims.others))
            root = jnp.concatenate(
                [roots_ref[:, i + 1].reshape(dims.columns, dims.block) for i in pair], axis=1
            )
            out_ref[rows, k * dims.block : (k + len(pair)) * dims.block] = dot(hot, root).astype(BF16)

    repeat_steps(dims.chunks, body)


def own_kernel(
    dims, roots_ref, cols_ref, message_ref, control_ref, obs_ref,
    model_ref, opt_ref, opw_ref, op_ref,
):
    half = lax.rem(lax.axis_index("var"), 2)
    bands = obs_ref.shape[0]
    flat = bands * dims.members
    vars_wide = as_bf16(
        within(iota((dims.lanes, dims.vars), 0) - dims.members * iota((dims.lanes, dims.vars), 1), 0, dims.members)
    )
    bands_wide = as_bf16(
        within(iota((bands, flat), 1) - dims.members * iota((bands, flat), 0), 0, dims.members)
    )
    opw = dot(dot_nt(vars_wide, obs_ref[...]).astype(BF16), bands_wide)
    same = lax.rem(iota(opw.shape, 0), dims.members) == lax.rem(iota(opw.shape, 1), dims.members)
    opw = jnp.where(same, opw, 0.0).astype(BF16)
    opw_ref[...] = opw
    spread, targets_of = scale_spread(dims, half), target_spread(dims)
    root = roots_ref[:, 0].reshape(dims.columns, dims.block)
    shift = ((1 - 2 * half) * dims.blocks).astype(F32)

    def body(step):
        rows = at(step, dims.chunk)
        wide = dims.others * dims.block
        plane = message_ref[rows, wide:]
        cols = column(cols_ref[at(step, dims.chunk_points), :])
        own = jnp.floor(cols * (1.0 / dims.block))
        targets = [jnp.broadcast_to(own, (dims.chunk, dims.block)).astype(BF16)]
        parts = [dot(one_hot(cols, dims.columns), root).astype(BF16)]
        ids = (dot(plane, targets_of) + shift).astype(BF16)
        for k in range(dims.others):
            lanes = slice(k * dims.block, (k + 1) * dims.block)
            targets.append(ids[:, lanes])
            parts.append(message_ref[rows, lanes])
        fill_operator(dims, op_ref, targets, parts)
        model = model_rows(dims, op_ref, plane, spread, control_ref, opw)
        if isinstance(step, int) and step == 0:
            model_ref[...] = model
        else:
            model_ref[...] += model
        opt_ref[:, rows] = op_ref[...].T

    if dims.chunks > 2:
        model_ref[...] = jnp.zeros_like(model_ref)
    repeat_steps(dims.chunks, body)


def side_parts(dims, message_ref, step, targets_of):
    rows = at(step, dims.chunk)
    wide = dims.others * dims.block
    plane = message_ref[rows, wide:]
    ids = dot(plane, targets_of).astype(BF16)
    lanes = [slice(k * dims.block, (k + 1) * dims.block) for k in range(dims.others)]
    return plane, [ids[:, l] for l in lanes], [message_ref[rows, l] for l in lanes]


def sides_kernel(dims, mine_ref, other_ref, own_ref, control_ref, opw_ref, keep_ref, give_ref, op_ref):
    half = lax.rem(lax.axis_index("var"), 2)
    spread, targets_of = scale_spread(dims, half), target_spread(dims)
    opw = opw_ref[...]
    give_ref[dims.slots :, :] = own_ref[...]
    for ref, model_ref in ((mine_ref, keep_ref), (other_ref, give_ref.at[: dims.slots])):

        def body(step):
            plane, targets, parts = side_parts(dims, ref, step, targets_of)
            fill_operator(dims, op_ref, targets, parts)
            model = model_rows(dims, op_ref, plane, spread, control_ref, opw)
            if isinstance(step, int) and step == 0:
                model_ref[...] = model
            else:
                model_ref[...] += model

        if dims.chunks > 2:
            model_ref[...] = jnp.zeros_like(model_ref)
        repeat_steps(dims.chunks, body)


def turn_kernel(dims, mine_ref, other_ref, opt_ref):
    targets_of = target_spread(dims)
    for side, ref in enumerate((mine_ref, other_ref)):

        def body(step):
            _, targets, parts = side_parts(dims, ref, step, targets_of)
            targets = [target.T for target in targets]
            parts = [part.T for part in parts]
            lanes = at(step + side * dims.chunks, dims.chunk)
            for q in range(dims.blocks):
                total = None
                for target, part in zip(targets, parts):
                    term = jnp.where(target == jnp.asarray(q, BF16), part, jnp.zeros((), BF16))
                    total = term if total is None else total + term
                opt_ref[q * dims.block : (q + 1) * dims.block, lanes] = total

        repeat_steps(dims.chunks, body)


def pull_rows(dims, pulled, scale):
    wide = scale.reshape(dims.chunk_points, dims.slots, dims.lanes) * pulled[None]
    return wide.reshape(dims.chunk, dims.lanes).astype(BF16)


def bands_to_vars(misfit, opw):
    high = misfit.astype(BF16)
    rest = misfit - high.astype(F32)
    middle = rest.astype(BF16)
    low = (rest - middle.astype(F32)).astype(BF16)
    return dot_nt(high, opw) + (dot_nt(middle, opw) + dot_nt(low, opw))


def own_adjoint_kernel(dims, misfit_ref, plane_ref, opt_ref, control_ref, opw_ref, out_ref, adj_ref):
    half = lax.rem(lax.axis_index("var"), 2)
    spread = scale_spread(dims, half)
    pulled = bands_to_vars(misfit_ref[...], opw_ref[...])

    def body(step):
        rows = at(step, dims.chunk)
        plane = plane_ref[rows, dims.others * dims.block :]
        adj_ref[rows, :] = pull_rows(dims, pulled, dot(plane, spread))

    repeat_steps(dims.chunks, body)
    for part in range(dims.columns // 256):
        rows = slice(part * 256, (part + 1) * 256)
        out_ref[rows, :] = control_ref[rows, :].astype(F32) + dot(opt_ref[rows, :], adj_ref[...])


def sides_adjoint_kernel(
    dims, misfit_ref, misfit2_ref, mine_ref, other_ref, opt_ref, own_ref, opw_ref, out_ref, adj_ref
):
    half = lax.rem(lax.axis_index("var"), 2)
    spread = scale_spread(dims, half)
    for side, (values_ref, ref) in enumerate(((misfit_ref, mine_ref), (misfit2_ref, other_ref))):
        pulled = bands_to_vars(values_ref[...], opw_ref[...])

        def body(step):
            scale = dot(ref[at(step, dims.chunk), dims.others * dims.block :], spread)
            adj_ref[at(step + side * dims.chunks, dims.chunk), :] = pull_rows(dims, pulled, scale)

        repeat_steps(dims.chunks, body)
    for part in range(dims.columns // 256):
        rows = slice(part * 256, (part + 1) * 256)
        total = own_ref[rows, :] + dot(opt_ref[rows, :], adj_ref[...])
        out_ref[rows, :] = total.astype(BF16)


class Dims:
    def __init__(self, control, roots, sigma, foot_cols):
        self.blocks, links, self.block = roots.shape[:3]
        self.others = links - 1
        self.columns, self.lanes = control.shape
        self.vars = sigma.shape[0]
        self.members = self.lanes // self.vars
        self.slots, self.points = foot_cols.shape
        self.rows = self.slots * self.points
        self.chunk_points = min(self.points, max(8, 512 // self.slots))
        self.chunk = self.chunk_points * self.slots
        self.chunks = self.rows // self.chunk
        self.width = self.others * self.block + LANES


def call(dims, kernel, name, out_shape, scratch, flops, limit=None):
    limit = (limit or min(56, max(16, dims.rows // 32))) * 1024 * 1024
    return pl.pallas_call(
        functools.partial(kernel, dims),
        out_shape=out_shape,
        scratch_shapes=scratch,
        compiler_params=pltpu.CompilerParams(vmem_limit_bytes=limit),
        cost_estimate=pl.CostEstimate(flops=flops, bytes_accessed=4000000, transcendentals=0),
        name=name,
    )


def shards(
    control,
    roots,
    neighbours,
    sigma,
    obs_op,
    foot_cols,
    foot_wgt,
    obs_value,
    obs_rinv,
    owner_counts,
):
    dims = Dims(control, roots, sigma, foot_cols)
    bands = obs_op.shape[1]
    members = dims.members
    tiles = lax.axis_size("space")
    ranks = lax.axis_size("var")
    outward, inward = [], []
    for t in range(tiles):
        for v in range(ranks):
            to = t + 1 - 2 * (v % 2)
            if 0 <= to < tiles:
                outward.append((t * ranks + v, to * ranks + v))
                inward.append((to * ranks + v, t * ranks + v))
    hop = lambda x, pairs: lax.ppermute(x, ("space", "var"), pairs)
    swap = lambda x, bit: lax.ppermute(x, "var", [(i, i ^ bit) for i in range(ranks)])
    shape = jax.ShapeDtypeStruct
    flat = bands * members
    cols_t, wgt_t = foot_cols.T, foot_wgt.T

    message = call(
        dims,
        select_kernel,
        "select",
        shape((dims.rows, dims.width), BF16),
        [],
        2000000000,
        56,
    )(roots, sigma, swap(sigma, 1), cols_t, wgt_t, neighbours)
    mine = hop(message, outward)

    message, obs_value, obs_rinv = lax.optimization_barrier((message, obs_value, obs_rinv))
    observed = lax.all_to_all(
        jnp.concatenate([obs_value, obs_rinv], axis=1), "space", 0, 0, tiled=True
    )
    capacity = dims.slots // owner_counts.shape[1]
    slot_ids = jnp.arange(dims.slots, dtype=jnp.int32)
    live = slot_ids % capacity < jnp.repeat(owner_counts[0], capacity)
    rinv = jnp.repeat(jnp.where(live[:, None], observed[:, flat:], 0.0), members, axis=1)
    value = observed[:, :flat]

    own_model, own_opt, opw = call(
        dims,
        own_kernel,
        "own_model",
        (
            shape((dims.slots, flat), F32),
            shape((dims.columns, dims.rows), BF16),
            shape((dims.lanes, flat), BF16),
        ),
        [pltpu.VMEM((dims.chunk, dims.columns), BF16)],
        4000000000,
    )(roots, cols_t, message, control, obs_op.T)

    mine, own_model, own_opt, rinv, value = lax.optimization_barrier(
        (mine, own_model, own_opt, rinv, value)
    )
    other = swap(mine, 1)
    keep, give = call(
        dims,
        sides_kernel,
        "sides_model",
        (shape((dims.slots, flat), F32), shape((2 * dims.slots, flat), F32)),
        [pltpu.VMEM((dims.chunk, dims.columns), BF16)],
        4000000000,
    )(mine, other, own_model, control, opw)
    got = swap(give, 1)
    arrived = hop(keep + got[: dims.slots], inward)
    sides_opt = call(
        dims,
        turn_kernel,
        "sides_turn",
        shape((dims.columns, 2 * dims.rows), BF16),
        [],
        4000000000,
    )(mine, other)
    arrived, sides_opt = lax.optimization_barrier((arrived, sides_opt))
    modelled = own_model + got[dims.slots :] + arrived + swap(arrived, 1)
    bit = 2
    while bit < ranks:
        modelled = modelled + swap(modelled, bit)
        bit *= 2
    misfit = rinv * (modelled - value)
    misfit_mine = hop(misfit, outward)

    own_total = call(
        dims,
        own_adjoint_kernel,
        "own_adjoint",
        shape((dims.columns, dims.lanes), F32),
        [pltpu.VMEM((dims.rows, dims.lanes), BF16)],
        2000000000,
    )(misfit, message, own_opt, control, opw)
    misfit_mine, own_total = lax.optimization_barrier((misfit_mine, own_total))
    misfit_other = swap(misfit_mine, 1)
    return call(
        dims,
        sides_adjoint_kernel,
        "sides_adjoint",
        shape((dims.columns, dims.lanes), BF16),
        [pltpu.VMEM((2 * dims.rows, dims.lanes), BF16)],
        4000000000,
    )(misfit_mine, misfit_other, mine, other, sides_opt, own_total, opw)


def solution(mesh):
    return jax.shard_map(
        shards,
        mesh=mesh,
        in_specs=(
            P("space", "var"),
            P("space", None, None, None),
            P("space", None),
            P("var", "space"),
            P("var", None),
            P("space", None),
            P("space", None),
            P("space", None),
            P("space", None),
            P("space", None),
        ),
        out_specs=P("space", "var"),
        check_vma=False,
    )
```

```python
import functools

import jax
import jax.numpy as jnp
from jax import lax
from jax.experimental import pallas as pl
from jax.experimental.pallas import tpu as pltpu
from jax.sharding import PartitionSpec as P

F32 = jnp.float32
BF16 = jnp.bfloat16
NT = (((1,), (1,)), ((), ()))


def repeat_steps(count, body):
    if count <= 2:
        for step in range(count):
            body(step)
    else:
        lax.fori_loop(0, count, lambda step, carry: (body(step), carry)[1], 0)


def at(step, size):
    if isinstance(step, int):
        return pl.ds(step * size, size)
    return pl.ds(pl.multiple_of(step * size, size), size)


def dot(a, b):
    return jnp.dot(a, b, preferred_element_type=F32)


def dot_nt(a, b):
    return lax.dot_general(a, b, NT, preferred_element_type=F32)


def iota(shape, axis):
    return lax.broadcasted_iota(jnp.int32, shape, axis)


def spread_rows(values):
    points, slots = values.shape
    wide = jnp.broadcast_to(values.astype(F32)[:, None, :], (points, slots, slots))
    wide = wide.reshape(points * slots, slots)
    hit = iota(wide.shape, 1) == lax.rem(iota(wide.shape, 0), slots)
    return jnp.where(hit, wide, 0.0)


def column(values):
    return jnp.sum(spread_rows(values), axis=1, keepdims=True)


def row_of(values):
    wide = spread_rows(values)
    high = wide.astype(BF16)
    low = (wide - high.astype(F32)).astype(BF16)
    ones = jnp.ones((8, wide.shape[1]), BF16)
    return (dot_nt(ones, high) + dot_nt(ones, low))[:1]


def one_hot(cols, count):
    lane = iota((cols.shape[0], count), 1)
    return jnp.where(lane == cols.astype(jnp.int32), 1.0, 0.0).astype(BF16)


def within(value, low, count):
    return (value >= low) & (value < low + count)


def as_bf16(mask):
    return jnp.where(mask, 1.0, 0.0).astype(BF16)


def scale_spread(dims, half):
    shape = (dims.plane, dims.lanes)
    row = iota(shape, 0) - dims.vars * half
    return as_bf16(within(iota(shape, 1) - dims.members * row, 0, dims.members))


def target_spread(dims):
    shape = (dims.plane, dims.width)
    row = iota(shape, 0) - 2 * dims.vars
    return as_bf16(within(iota(shape, 1) - dims.block * row, 0, dims.block))


def plane_of(dims, message_ref, step):
    pieces = []
    for i in range(dims.chunk // dims.width):
        pieces.append(message_ref[at(step * (dims.chunk // dims.width) + i, dims.plane), :])
    return pieces[0] if len(pieces) == 1 else jnp.concatenate(pieces, axis=1)


def roots_of(dims, message_ref, step):
    rows = pl.ds(dims.head + step * dims.chunk, dims.chunk)
    if not isinstance(step, int):
        rows = pl.ds(pl.multiple_of(dims.head + step * dims.chunk, 64), dims.chunk)
    return [
        message_ref[rows, k * dims.block : (k + 1) * dims.block] for k in range(dims.others)
    ]


def fill_operator(dims, op_ref, targets, parts):
    for q in range(dims.blocks):
        total = None
        for target, part in zip(targets, parts):
            term = jnp.where(target == jnp.asarray(q, target.dtype), part, jnp.zeros((), part.dtype))
            total = term if total is None else total + term
        op_ref[:, q * dims.block : (q + 1) * dims.block] = total


def model_rows(dims, op_ref, scale, control_ref, opw):
    summed = dot(op_ref[...], control_ref[...])
    state = (summed * scale).astype(BF16)
    bands = dot(state, opw)
    return jnp.sum(bands.reshape(dims.chunk_points, dims.slots, bands.shape[1]), axis=0)


def select_kernel(dims, roots_ref, sigma_ref, sigma2_ref, cols_ref, wgt_ref, nb_ref, out_ref):
    tile = lax.axis_index("space")
    half = lax.rem(lax.axis_index("var"), 2)
    sigma, sigma2 = sigma_ref[...], sigma2_ref[...]
    sigma = jnp.concatenate(
        [jnp.where(half == 0, sigma, sigma2), jnp.where(half == 0, sigma2, sigma)], axis=0
    )
    high = sigma.astype(BF16).astype(F32)
    nb = nb_ref[...] + ((2 * half - 1) - tile) * dims.blocks
    nb = nb.astype(F32)
    base = 2 * dims.vars
    ids = jnp.zeros((dims.plane - base, dims.columns), F32)
    shape = ids.shape
    for b in range(dims.blocks):
        in_block = within(iota(shape, 1), b * dims.block, dims.block)
        for k in range(dims.others):
            ids = jnp.where(in_block & (iota(shape, 0) == k), nb[b : b + 1, k + 1 : k + 2], ids)
    rest = jnp.zeros_like(ids)
    table = jnp.concatenate([high, ids, sigma - high, rest], axis=0).astype(BF16)

    def body(step):
        points = at(step, dims.chunk_points)
        hot = one_hot(column(cols_ref[points, :]), dims.columns)
        plane = dot_nt(table, hot)
        scale = (plane[:base] + plane[dims.plane : dims.plane + base]) * row_of(wgt_ref[points, :])
        plane = jnp.concatenate([scale, plane[base : dims.plane]], axis=0).astype(BF16)
        pieces = dims.chunk // dims.width
        for i in range(pieces):
            out_ref[at(step * pieces + i, dims.plane), :] = plane[
                :, i * dims.width : (i + 1) * dims.width
            ]
        rows = pl.ds(dims.head + step * dims.chunk, dims.chunk)
        if not isinstance(step, int):
            rows = pl.ds(pl.multiple_of(dims.head + step * dims.chunk, 64), dims.chunk)
        for k in range(0, dims.others, 2):
            pair = range(k, min(k + 2, dims.others))
            root = jnp.concatenate(
                [roots_ref[:, i + 1].reshape(dims.columns, dims.block) for i in pair], axis=1
            )
            out_ref[rows, k * dims.block : (k + len(pair)) * dims.block] = dot(hot, root).astype(BF16)

    repeat_steps(dims.chunks, body)


def own_kernel(
    dims, roots_ref, cols_ref, message_ref, control_ref, obs_ref,
    model_ref, opt_ref, opw_ref, op_ref,
):
    half = lax.rem(lax.axis_index("var"), 2)
    bands = obs_ref.shape[0]
    flat = bands * dims.members
    vars_wide = as_bf16(
        within(iota((dims.lanes, dims.vars), 0) - dims.members * iota((dims.lanes, dims.vars), 1), 0, dims.members)
    )
    bands_wide = as_bf16(
        within(iota((bands, flat), 1) - dims.members * iota((bands, flat), 0), 0, dims.members)
    )
    opw = dot(dot_nt(vars_wide, obs_ref[...]).astype(BF16), bands_wide)
    same = lax.rem(iota(opw.shape, 0), dims.members) == lax.rem(iota(opw.shape, 1), dims.members)
    opw = jnp.where(same, opw, 0.0).astype(BF16)
    opw_ref[...] = opw
    spread, targets_of = scale_spread(dims, half), target_spread(dims)
    root = roots_ref[:, 0].reshape(dims.columns, dims.block)
    shift = ((1 - 2 * half) * dims.blocks).astype(F32)

    def body(step):
        rows = at(step, dims.chunk)
        plane = plane_of(dims, message_ref, step).T
        cols = column(cols_ref[at(step, dims.chunk_points), :])
        own = jnp.floor(cols * (1.0 / dims.block))
        targets = [jnp.broadcast_to(own, (dims.chunk, dims.block)).astype(BF16)]
        parts = [dot(one_hot(cols, dims.columns), root).astype(BF16)]
        ids = (dot(plane, targets_of) + shift).astype(BF16)
        for k in range(dims.others):
            targets.append(ids[:, k * dims.block : (k + 1) * dims.block])
        parts += roots_of(dims, message_ref, step)
        fill_operator(dims, op_ref, targets, parts)
        model = model_rows(dims, op_ref, dot(plane, spread), control_ref, opw)
        if isinstance(step, int) and step == 0:
            model_ref[...] = model
        else:
            model_ref[...] += model
        opt_ref[:, rows] = op_ref[...].T

    if dims.chunks > 2:
        model_ref[...] = jnp.zeros_like(model_ref)
    repeat_steps(dims.chunks, body)


def side_kernel(dims, message_ref, control_ref, opw_ref, model_ref, op_ref):
    half = lax.rem(lax.axis_index("var"), 2)
    spread, targets_of = scale_spread(dims, half), target_spread(dims)
    opw = opw_ref[...]

    def body(step):
        plane = plane_of(dims, message_ref, step).T
        ids = dot(plane, targets_of).astype(BF16)
        targets = [ids[:, k * dims.block : (k + 1) * dims.block] for k in range(dims.others)]
        fill_operator(dims, op_ref, targets, roots_of(dims, message_ref, step))
        model = model_rows(dims, op_ref, dot(plane, spread), control_ref, opw)
        if isinstance(step, int) and step == 0:
            model_ref[...] = model
        else:
            model_ref[...] += model

    if dims.chunks > 2:
        model_ref[...] = jnp.zeros_like(model_ref)
    repeat_steps(dims.chunks, body)


def give_kernel(dims, message_ref, own_ref, control_ref, opw_ref, give_ref, op_ref):
    give_ref[dims.slots :, :] = own_ref[...]
    side_kernel(dims, message_ref, control_ref, opw_ref, give_ref.at[: dims.slots], op_ref)


def turn_kernel(dims, mine_ref, other_ref, mine_opt_ref, other_opt_ref):
    for ref, opt_ref in ((mine_ref, mine_opt_ref), (other_ref, other_opt_ref)):

        def body(step):
            plane = plane_of(dims, ref, step).astype(F32)
            parts = [part.T for part in roots_of(dims, ref, step)]
            targets = []
            for k in range(dims.others):
                row = plane[2 * dims.vars + k : 2 * dims.vars + k + 1]
                targets.append(jnp.broadcast_to(row, (dims.block, dims.chunk)).astype(BF16))
            for q in range(dims.blocks):
                total = None
                for target, part in zip(targets, parts):
                    term = jnp.where(target == jnp.asarray(q, BF16), part, jnp.zeros((), BF16))
                    total = term if total is None else total + term
                opt_ref[q * dims.block : (q + 1) * dims.block, at(step, dims.chunk)] = total

        repeat_steps(dims.chunks, body)


def adjoint_kernel(dims, misfit_ref, message_ref, opt_ref, base_ref, opw_ref, out_ref, adj_ref):
    half = lax.rem(lax.axis_index("var"), 2)
    spread = scale_spread(dims, half)
    misfit, opw = misfit_ref[...], opw_ref[...]
    high = misfit.astype(BF16)
    rest = misfit - high.astype(F32)
    middle = rest.astype(BF16)
    low = (rest - middle.astype(F32)).astype(BF16)
    pulled = dot_nt(high, opw) + (dot_nt(middle, opw) + dot_nt(low, opw))

    def body(step):
        scale = dot(plane_of(dims, message_ref, step).T, spread)
        wide = scale.reshape(dims.chunk_points, dims.slots, dims.lanes) * pulled[None]
        adj_ref[at(step, dims.chunk), :] = wide.reshape(dims.chunk, dims.lanes).astype(BF16)

    repeat_steps(dims.chunks, body)
    for part in range(dims.columns // 256):
        rows = slice(part * 256, (part + 1) * 256)
        total = base_ref[rows, :].astype(F32) + dot(opt_ref[rows, :], adj_ref[...])
        out_ref[rows, :] = total.astype(out_ref.dtype)


class Dims:
    def __init__(self, control, roots, sigma, foot_cols):
        self.blocks, links, self.block = roots.shape[:3]
        self.others = links - 1
        self.columns, self.lanes = control.shape
        self.vars = sigma.shape[0]
        self.members = self.lanes // self.vars
        self.slots, self.points = foot_cols.shape
        self.rows = self.slots * self.points
        self.chunk_points = min(self.points, max(8, 512 // self.slots))
        self.chunk = self.chunk_points * self.slots
        self.chunks = self.rows // self.chunk
        self.width = self.others * self.block
        self.plane = 64
        self.head = self.plane * (self.rows // self.width)


def call(dims, kernel, name, out_shape, scratch, flops, limit=None):
    limit = (limit or min(56, max(16, dims.rows // 32))) * 1024 * 1024
    return pl.pallas_call(
        functools.partial(kernel, dims),
        out_shape=out_shape,
        scratch_shapes=scratch,
        compiler_params=pltpu.CompilerParams(vmem_limit_bytes=limit),
        cost_estimate=pl.CostEstimate(flops=flops, bytes_accessed=4000000, transcendentals=0),
        name=name,
    )


def shards(
    control,
    roots,
    neighbours,
    sigma,
    obs_op,
    foot_cols,
    foot_wgt,
    obs_value,
    obs_rinv,
    owner_counts,
):
    dims = Dims(control, roots, sigma, foot_cols)
    bands = obs_op.shape[1]
    members = dims.members
    tiles = lax.axis_size("space")
    ranks = lax.axis_size("var")
    outward, inward = [], []
    for t in range(tiles):
        for v in range(ranks):
            to = t + 1 - 2 * (v % 2)
            if 0 <= to < tiles:
                outward.append((t * ranks + v, to * ranks + v))
                inward.append((to * ranks + v, t * ranks + v))
    hop = lambda x, pairs: lax.ppermute(x, ("space", "var"), pairs)
    swap = lambda x, bit: lax.ppermute(x, "var", [(i, i ^ bit) for i in range(ranks)])
    shape = jax.ShapeDtypeStruct
    flat = bands * members
    cols_t, wgt_t = foot_cols.T, foot_wgt.T

    message = call(
        dims,
        select_kernel,
        "select",
        shape((dims.head + dims.rows, dims.width), BF16),
        [],
        2000000000,
        56,
    )(roots, sigma, swap(sigma, 1), cols_t, wgt_t, neighbours)
    mine = hop(message, outward)

    message, obs_value, obs_rinv, owner_counts = lax.optimization_barrier(
        (message, obs_value, obs_rinv, owner_counts)
    )
    observed = lax.all_to_all(
        jnp.concatenate([obs_value, obs_rinv], axis=1), "space", 0, 0, tiled=True
    )
    capacity = dims.slots // owner_counts.shape[1]
    slot_ids = jnp.arange(dims.slots, dtype=jnp.int32)
    live = slot_ids % capacity < jnp.repeat(owner_counts[0], capacity)
    rinv = jnp.repeat(jnp.where(live[:, None], observed[:, flat:], 0.0), members, axis=1)
    value = observed[:, :flat]

    own_model, own_opt, opw = call(
        dims,
        own_kernel,
        "own_model",
        (
            shape((dims.slots, flat), F32),
            shape((dims.columns, dims.rows), BF16),
            shape((dims.lanes, flat), BF16),
        ),
        [pltpu.VMEM((dims.chunk, dims.columns), BF16)],
        4000000000,
    )(roots, cols_t, message, control, obs_op.T)

    mine, own_model, own_opt, rinv, value = lax.optimization_barrier(
        (mine, own_model, own_opt, rinv, value)
    )
    other = swap(mine, 1)
    op_scratch = [pltpu.VMEM((dims.chunk, dims.columns), BF16)]
    keep = call(
        dims, side_kernel, "mine_model", shape((dims.slots, flat), F32), op_scratch, 2000000000
    )(mine, control, opw)
    other, keep = lax.optimization_barrier((other, keep))
    give = call(
        dims, give_kernel, "other_model", shape((2 * dims.slots, flat), F32), op_scratch, 2000000000
    )(other, own_model, control, opw)
    got = swap(give, 1)
    arrived = hop(keep + got[: dims.slots], inward)
    mine_opt, other_opt = call(
        dims,
        turn_kernel,
        "sides_turn",
        (shape((dims.columns, dims.rows), BF16),) * 2,
        [],
        4000000000,
    )(mine, other)
    arrived, mine_opt, other_opt = lax.optimization_barrier((arrived, mine_opt, other_opt))
    modelled = own_model + got[dims.slots :] + arrived + swap(arrived, 1)
    bit = 2
    while bit < ranks:
        modelled = modelled + swap(modelled, bit)
        bit *= 2
    misfit = rinv * (modelled - value)
    misfit_mine = hop(misfit, outward)

    def add_adjoint(name, dtype, *operands):
        return call(
            dims,
            adjoint_kernel,
            name,
            shape((dims.columns, dims.lanes), dtype),
            [pltpu.VMEM((dims.rows, dims.lanes), BF16)],
            2000000000,
        )(*operands, opw)

    total = add_adjoint("own_adjoint", F32, misfit, message, own_opt, control)
    misfit_mine, total = lax.optimization_barrier((misfit_mine, total))
    misfit_other = swap(misfit_mine, 1)
    total = add_adjoint("mine_adjoint", F32, misfit_mine, mine, mine_opt, total)
    misfit_other, total = lax.optimization_barrier((misfit_other, total))
    return add_adjoint("other_adjoint", BF16, misfit_other, other, other_opt, total)


def solution(mesh):
    return jax.shard_map(
        shards,
        mesh=mesh,
        in_specs=(
            P("space", "var"),
            P("space", None, None, None),
            P("space", None),
            P("var", "space"),
            P("var", None),
            P("space", None),
            P("space", None),
            P("space", None),
            P("space", None),
            P("space", None),
        ),
        out_specs=P("space", "var"),
        check_vma=False,
    )
```

```python
import functools

import jax
import jax.numpy as jnp
from jax import lax
from jax.experimental import pallas as pl
from jax.experimental.pallas import tpu as pltpu
from jax.sharding import PartitionSpec as P

F32 = jnp.float32
BF16 = jnp.bfloat16
NT = (((1,), (1,)), ((), ()))


def repeat_steps(count, body):
    if count <= 2:
        for step in range(count):
            body(step)
    else:
        lax.fori_loop(0, count, lambda step, carry: (body(step), carry)[1], 0)


def at(step, size):
    if isinstance(step, int):
        return pl.ds(step * size, size)
    return pl.ds(pl.multiple_of(step * size, size), size)


def dot(a, b):
    return jnp.dot(a, b, preferred_element_type=F32)


def dot_nt(a, b):
    return lax.dot_general(a, b, NT, preferred_element_type=F32)


def iota(shape, axis):
    return lax.broadcasted_iota(jnp.int32, shape, axis)


def spread_rows(values):
    points, slots = values.shape
    wide = jnp.broadcast_to(values.astype(F32)[:, None, :], (points, slots, slots))
    wide = wide.reshape(points * slots, slots)
    hit = iota(wide.shape, 1) == lax.rem(iota(wide.shape, 0), slots)
    return jnp.where(hit, wide, 0.0)


def column(values):
    return jnp.sum(spread_rows(values), axis=1, keepdims=True)


def row_of(values):
    wide = spread_rows(values)
    high = wide.astype(BF16)
    low = (wide - high.astype(F32)).astype(BF16)
    ones = jnp.ones((8, wide.shape[1]), BF16)
    return (dot_nt(ones, high) + dot_nt(ones, low))[:1]


def one_hot(cols, count):
    lane = iota((cols.shape[0], count), 1)
    return jnp.where(lane == cols.astype(jnp.int32), 1.0, 0.0).astype(BF16)


def within(value, low, count):
    return (value >= low) & (value < low + count)


def as_bf16(mask):
    return jnp.where(mask, 1.0, 0.0).astype(BF16)


def scale_spread(dims, half):
    shape = (dims.plane, dims.lanes)
    row = iota(shape, 0) - dims.vars * half
    return as_bf16(within(iota(shape, 1) - dims.members * row, 0, dims.members))


def target_spread(dims):
    shape = (dims.plane, dims.width)
    row = iota(shape, 0) - 2 * dims.vars
    return as_bf16(within(iota(shape, 1) - dims.block * row, 0, dims.block))


def roots_of(dims, rows_ref, step):
    rows = at(step, dims.chunk)
    return [rows_ref[rows, k * dims.block : (k + 1) * dims.block] for k in range(dims.others)]


def fill_operator(dims, op_ref, targets, parts):
    for q in range(dims.blocks):
        total = None
        for target, part in zip(targets, parts):
            term = jnp.where(target == jnp.asarray(q, target.dtype), part, jnp.zeros((), part.dtype))
            total = term if total is None else total + term
        op_ref[:, q * dims.block : (q + 1) * dims.block] = total


def model_rows(dims, op_ref, scale, control_ref, opw):
    summed = dot(op_ref[...], control_ref[...])
    state = (summed * scale).astype(BF16)
    bands = dot(state, opw)
    return jnp.sum(bands.reshape(dims.chunk_points, dims.slots, bands.shape[1]), axis=0)


def partner_step(tile, rank):
    return (1 - 2 * lax.rem(tile, 2)) * (1 - 2 * lax.rem(rank, 2))


def select_kernel(dims, roots_ref, cols_ref, out_ref):
    def body(step):
        hot = one_hot(column(cols_ref[at(step, dims.chunk_points), :]), dims.columns)
        for k in range(0, dims.others, 2):
            pair = range(k, min(k + 2, dims.others))
            root = jnp.concatenate(
                [roots_ref[:, i + 1].reshape(dims.columns, dims.block) for i in pair], axis=1
            )
            lanes = slice(k * dims.block, (k + len(pair)) * dims.block)
            out_ref[at(step, dims.chunk), lanes] = dot(hot, root).astype(BF16)

    repeat_steps(dims.chunks, body)


def plane_kernel(
    dims, sigma_ref, sigma2_ref, cols_ref, wgt_ref, nb_ref, obs_ref, plane_ref, opw_ref
):
    tile = lax.axis_index("space")
    half = lax.rem(lax.axis_index("var"), 2)
    bands = obs_ref.shape[0]
    flat = bands * dims.members
    shape = (dims.lanes, dims.vars)
    vars_wide = as_bf16(within(iota(shape, 0) - dims.members * iota(shape, 1), 0, dims.members))
    shape = (bands, flat)
    bands_wide = as_bf16(within(iota(shape, 1) - dims.members * iota(shape, 0), 0, dims.members))
    opw = dot(dot_nt(vars_wide, obs_ref[...]).astype(BF16), bands_wide)
    same = lax.rem(iota(opw.shape, 0), dims.members) == lax.rem(iota(opw.shape, 1), dims.members)
    opw_ref[...] = jnp.where(same, opw, 0.0).astype(BF16)
    sigma, sigma2 = sigma_ref[...], sigma2_ref[...]
    sigma = jnp.concatenate(
        [jnp.where(half == 0, sigma, sigma2), jnp.where(half == 0, sigma2, sigma)], axis=0
    )
    high = sigma.astype(BF16).astype(F32)
    nb = nb_ref[...] - (tile + partner_step(tile, half)) * dims.blocks
    nb = nb.astype(F32)
    base = 2 * dims.vars
    ids = jnp.zeros((dims.plane - base, dims.columns), F32)
    shape = ids.shape
    for b in range(dims.blocks):
        in_block = within(iota(shape, 1), b * dims.block, dims.block)
        for k in range(dims.others):
            ids = jnp.where(in_block & (iota(shape, 0) == k), nb[b : b + 1, k + 1 : k + 2], ids)
    rest = jnp.zeros_like(ids)
    table = jnp.concatenate([high, ids, sigma - high, rest], axis=0).astype(BF16)

    def body(step):
        points = at(step, dims.chunk_points)
        hot = one_hot(column(cols_ref[points, :]), dims.columns)
        plane = dot_nt(table, hot)
        scale = (plane[:base] + plane[dims.plane : dims.plane + base]) * row_of(wgt_ref[points, :])
        plane = jnp.concatenate([scale, plane[base : dims.plane]], axis=0).astype(BF16)
        plane_ref[:, at(step, dims.chunk)] = plane

    repeat_steps(dims.chunks, body)


def own_kernel(
    dims, roots_ref, cols_ref, rows_ref, plane_ref, control_ref, opw_ref, model_ref, opt_ref, op_ref
):
    half = lax.rem(lax.axis_index("var"), 2)
    opw = opw_ref[...]
    spread, targets_of = scale_spread(dims, half), target_spread(dims)
    root = roots_ref[:, 0].reshape(dims.columns, dims.block)
    shift = (partner_step(lax.axis_index("space"), half) * dims.blocks).astype(F32)

    def body(step):
        rows = at(step, dims.chunk)
        plane = plane_ref[:, rows].T
        cols = column(cols_ref[at(step, dims.chunk_points), :])
        own = jnp.floor(cols * (1.0 / dims.block))
        targets = [jnp.broadcast_to(own, (dims.chunk, dims.block)).astype(BF16)]
        parts = [dot(one_hot(cols, dims.columns), root).astype(BF16)]
        ids = (dot(plane, targets_of) + shift).astype(BF16)
        for k in range(dims.others):
            targets.append(ids[:, k * dims.block : (k + 1) * dims.block])
        parts += roots_of(dims, rows_ref, step)
        fill_operator(dims, op_ref, targets, parts)
        model = model_rows(dims, op_ref, dot(plane, spread), control_ref, opw)
        if isinstance(step, int) and step == 0:
            model_ref[...] = model
        else:
            model_ref[...] += model
        opt_ref[:, rows] = op_ref[...].T

    if dims.chunks > 2:
        model_ref[...] = jnp.zeros_like(model_ref)
    repeat_steps(dims.chunks, body)


def side_kernel(dims, rows_ref, plane_ref, control_ref, opw_ref, model_ref, op_ref):
    half = lax.rem(lax.axis_index("var"), 2)
    spread, targets_of = scale_spread(dims, half), target_spread(dims)
    opw = opw_ref[...]

    def body(step):
        plane = plane_ref[:, at(step, dims.chunk)].T
        ids = dot(plane, targets_of).astype(BF16)
        targets = [ids[:, k * dims.block : (k + 1) * dims.block] for k in range(dims.others)]
        fill_operator(dims, op_ref, targets, roots_of(dims, rows_ref, step))
        model = model_rows(dims, op_ref, dot(plane, spread), control_ref, opw)
        if isinstance(step, int) and step == 0:
            model_ref[...] = model
        else:
            model_ref[...] += model

    if dims.chunks > 2:
        model_ref[...] = jnp.zeros_like(model_ref)
    repeat_steps(dims.chunks, body)


def fill_turned(dims, opt_ref, rows_ref, plane_ref):
    def body(step):
        plane = plane_ref[:, at(step, dims.chunk)].astype(F32)
        parts = [part.T for part in roots_of(dims, rows_ref, step)]
        targets = []
        for k in range(dims.others):
            row = plane[2 * dims.vars + k : 2 * dims.vars + k + 1]
            targets.append(jnp.broadcast_to(row, (dims.block, dims.chunk)).astype(BF16))
        for q in range(dims.blocks):
            total = None
            for target, part in zip(targets, parts):
                term = jnp.where(target == jnp.asarray(q, BF16), part, jnp.zeros((), BF16))
                total = term if total is None else total + term
            opt_ref[q * dims.block : (q + 1) * dims.block, at(step, dims.chunk)] = total

    repeat_steps(dims.chunks, body)


def adjoint_kernel(dims, misfit_ref, plane_ref, opt_ref, base_ref, opw_ref, out_ref, adj_ref):
    half = lax.rem(lax.axis_index("var"), 2)
    spread = scale_spread(dims, half)
    misfit, opw = misfit_ref[...], opw_ref[...]
    high = misfit.astype(BF16)
    rest = misfit - high.astype(F32)
    middle = rest.astype(BF16)
    low = (rest - middle.astype(F32)).astype(BF16)
    pulled = dot_nt(high, opw) + (dot_nt(middle, opw) + dot_nt(low, opw))

    def body(step):
        scale = dot(plane_ref[:, at(step, dims.chunk)].T, spread)
        wide = scale.reshape(dims.chunk_points, dims.slots, dims.lanes) * pulled[None]
        adj_ref[at(step, dims.chunk), :] = wide.reshape(dims.chunk, dims.lanes).astype(BF16)

    repeat_steps(dims.chunks, body)
    for part in range(dims.columns // 256):
        rows = slice(part * 256, (part + 1) * 256)
        total = base_ref[rows, :].astype(F32) + dot(opt_ref[rows, :], adj_ref[...])
        out_ref[rows, :] = total.astype(out_ref.dtype)


def side_adjoint_kernel(
    dims, misfit_ref, plane_ref, rows_ref, base_ref, opw_ref, out_ref, adj_ref, opt_ref
):
    fill_turned(dims, opt_ref, rows_ref, plane_ref)
    adjoint_kernel(dims, misfit_ref, plane_ref, opt_ref, base_ref, opw_ref, out_ref, adj_ref)


class Dims:
    def __init__(self, control, roots, sigma, foot_cols):
        self.blocks, links, self.block = roots.shape[:3]
        self.others = links - 1
        self.columns, self.lanes = control.shape
        self.vars = sigma.shape[0]
        self.members = self.lanes // self.vars
        self.slots, self.points = foot_cols.shape
        self.rows = self.slots * self.points
        self.chunk_points = min(self.points, max(8, 512 // self.slots))
        self.chunk = self.chunk_points * self.slots
        self.chunks = self.rows // self.chunk
        self.width = self.others * self.block
        self.plane = 64


def call(dims, kernel, name, out_shape, scratch, flops, limit=None):
    limit = (limit or min(56, max(16, dims.rows // 32))) * 1024 * 1024
    return pl.pallas_call(
        functools.partial(kernel, dims),
        out_shape=out_shape,
        scratch_shapes=scratch,
        compiler_params=pltpu.CompilerParams(vmem_limit_bytes=limit),
        cost_estimate=pl.CostEstimate(flops=flops, bytes_accessed=4000000, transcendentals=0),
        name=name,
    )


def shards(
    control,
    roots,
    neighbours,
    sigma,
    obs_op,
    foot_cols,
    foot_wgt,
    obs_value,
    obs_rinv,
    owner_counts,
):
    dims = Dims(control, roots, sigma, foot_cols)
    bands = obs_op.shape[1]
    members = dims.members
    tiles = lax.axis_size("space")
    ranks = lax.axis_size("var")
    partners = []
    for t in range(tiles):
        for v in range(ranks):
            to = t + (1 - 2 * (t % 2)) * (1 - 2 * (v % 2))
            if 0 <= to < tiles:
                partners.append((t * ranks + v, to * ranks + v))
    hop = lambda x: lax.ppermute(x, ("space", "var"), partners)
    swap = lambda x, bit: lax.ppermute(x, "var", [(i, i ^ bit) for i in range(ranks)])
    shape = jax.ShapeDtypeStruct
    flat = bands * members
    cols_t, wgt_t = foot_cols.T, foot_wgt.T

    sigma2 = swap(sigma, 1)
    picked = call(
        dims, select_kernel, "select", shape((dims.rows, dims.width), BF16), [], 2000000000, 56
    )(roots, cols_t)
    mine = hop(picked)
    picked, sigma2 = lax.optimization_barrier((picked, sigma2))
    plane, opw = call(
        dims,
        plane_kernel,
        "plane",
        (shape((dims.plane, dims.rows), BF16), shape((dims.lanes, flat), BF16)),
        [],
        1000000000,
    )(sigma, sigma2, cols_t, wgt_t, neighbours, obs_op.T)
    mine_plane = hop(plane)
    plane, obs_value, obs_rinv, owner_counts = lax.optimization_barrier(
        (plane, obs_value, obs_rinv, owner_counts)
    )
    observed = lax.all_to_all(
        jnp.concatenate([obs_value, obs_rinv], axis=1), "space", 0, 0, tiled=True
    )
    capacity = dims.slots // owner_counts.shape[1]
    slot_ids = jnp.arange(dims.slots, dtype=jnp.int32)
    live = slot_ids % capacity < jnp.repeat(owner_counts[0], capacity)
    rinv = jnp.repeat(jnp.where(live[:, None], observed[:, flat:], 0.0), members, axis=1)
    value = observed[:, :flat]

    mine, mine_plane, rinv, value = lax.optimization_barrier((mine, mine_plane, rinv, value))
    other, other_plane = swap(mine, 1), swap(mine_plane, 1)
    op_scratch = [pltpu.VMEM((dims.chunk, dims.columns), BF16)]
    keep = call(
        dims, side_kernel, "mine_model", shape((dims.slots, flat), F32), op_scratch, 2000000000
    )(mine, mine_plane, control, opw)
    other, keep = lax.optimization_barrier((other, keep))
    give = call(
        dims, side_kernel, "other_model", shape((dims.slots, flat), F32), op_scratch, 2000000000
    )(other, other_plane, control, opw)
    arrived = hop(keep + swap(give, 1))
    give, own_picked = lax.optimization_barrier((give, picked))
    own_model, own_opt = call(
        dims,
        own_kernel,
        "own_model",
        (shape((dims.slots, flat), F32), shape((dims.columns, dims.rows), BF16)),
        op_scratch,
        4000000000,
    )(roots, cols_t, own_picked, plane, control, opw)
    arrived, own_model, own_opt = lax.optimization_barrier((arrived, own_model, own_opt))
    modelled = arrived + own_model
    bit = 1
    while bit < ranks:
        modelled = modelled + swap(modelled, bit)
        bit *= 2
    misfit = rinv * (modelled - value)
    misfit_mine = hop(misfit)

    def add_adjoint(kernel, name, dtype, scratch, *operands):
        return call(
            dims,
            kernel,
            name,
            shape((dims.columns, dims.lanes), dtype),
            [pltpu.VMEM((dims.rows, dims.lanes), BF16)] + scratch,
            2000000000,
        )(*operands, opw)

    total = add_adjoint(
        adjoint_kernel, "own_adjoint", F32, [], misfit, plane, own_opt, control
    )
    misfit_mine, total = lax.optimization_barrier((misfit_mine, total))
    misfit_other = swap(misfit_mine, 1)
    turned = [pltpu.VMEM((dims.columns, dims.rows), BF16)]
    total = add_adjoint(
        side_adjoint_kernel, "mine_adjoint", F32, turned, misfit_mine, mine_plane, mine, total
    )
    misfit_other, total = lax.optimization_barrier((misfit_other, total))
    return add_adjoint(
        side_adjoint_kernel, "other_adjoint", BF16, turned, misfit_other, other_plane, other, total
    )


def solution(mesh):
    return jax.shard_map(
        shards,
        mesh=mesh,
        in_specs=(
            P("space", "var"),
            P("space", None, None, None),
            P("space", None),
            P("var", "space"),
            P("var", None),
            P("space", None),
            P("space", None),
            P("space", None),
            P("space", None),
            P("space", None),
        ),
        out_specs=P("space", "var"),
        check_vma=False,
    )
```

```python
import functools

import jax
import jax.numpy as jnp
from jax import lax
from jax.experimental import pallas as pl
from jax.experimental.pallas import tpu as pltpu
from jax.sharding import PartitionSpec as P

F32 = jnp.float32
BF16 = jnp.bfloat16
NT = (((1,), (1,)), ((), ()))


def repeat_steps(count, body):
    if count <= 2:
        for step in range(count):
            body(step)
    else:
        lax.fori_loop(0, count, lambda step, carry: (body(step), carry)[1], 0)


def at(step, size):
    if isinstance(step, int):
        return pl.ds(step * size, size)
    return pl.ds(pl.multiple_of(step * size, size), size)


def dot(a, b):
    return jnp.dot(a, b, preferred_element_type=F32)


def dot_nt(a, b):
    return lax.dot_general(a, b, NT, preferred_element_type=F32)


def iota(shape, axis):
    return lax.broadcasted_iota(jnp.int32, shape, axis)


def spread_rows(values):
    points, slots = values.shape
    wide = jnp.broadcast_to(values.astype(F32)[:, None, :], (points, slots, slots))
    wide = wide.reshape(points * slots, slots)
    hit = iota(wide.shape, 1) == lax.rem(iota(wide.shape, 0), slots)
    return jnp.where(hit, wide, 0.0)


def column(values):
    return jnp.sum(spread_rows(values), axis=1, keepdims=True)


def row_of(values):
    wide = spread_rows(values)
    high = wide.astype(BF16)
    low = (wide - high.astype(F32)).astype(BF16)
    ones = jnp.ones((8, wide.shape[1]), BF16)
    return (dot_nt(ones, high) + dot_nt(ones, low))[:1]


def one_hot(cols, count):
    lane = iota((cols.shape[0], count), 1)
    return jnp.where(lane == cols.astype(jnp.int32), 1.0, 0.0).astype(BF16)


def within(value, low, count):
    return (value >= low) & (value < low + count)


def as_bf16(mask):
    return jnp.where(mask, 1.0, 0.0).astype(BF16)


def scale_spread(dims, half):
    shape = (dims.plane, dims.lanes)
    row = iota(shape, 0) - dims.vars * half
    return as_bf16(within(iota(shape, 1) - dims.members * row, 0, dims.members))


def target_spread(dims):
    shape = (dims.plane, dims.width)
    row = iota(shape, 0) - 2 * dims.vars
    return as_bf16(within(iota(shape, 1) - dims.block * row, 0, dims.block))


def roots_of(dims, rows_ref, step):
    rows = at(step, dims.chunk)
    return [rows_ref[rows, k * dims.block : (k + 1) * dims.block] for k in range(dims.others)]


def fill_operator(dims, op_ref, targets, parts):
    for q in range(dims.blocks):
        total = None
        for target, part in zip(targets, parts):
            term = jnp.where(target == jnp.asarray(q, target.dtype), part, jnp.zeros((), part.dtype))
            total = term if total is None else total + term
        op_ref[:, q * dims.block : (q + 1) * dims.block] = total


def model_rows(dims, op_ref, scale, control_ref, opw):
    summed = dot(op_ref[...], control_ref[...])
    state = (summed * scale).astype(BF16)
    bands = dot(state, opw)
    return jnp.sum(bands.reshape(dims.chunk_points, dims.slots, bands.shape[1]), axis=0)


def partner_step(tile, rank):
    return (1 - 2 * lax.rem(tile, 2)) * (1 - 2 * lax.rem(rank, 2))


def select_kernel(dims, roots_ref, cols_ref, out_ref):
    def body(step):
        hot = one_hot(column(cols_ref[at(step, dims.chunk_points), :]), dims.columns)
        for k in range(0, dims.others, 2):
            pair = range(k, min(k + 2, dims.others))
            root = jnp.concatenate(
                [roots_ref[:, i + 1].reshape(dims.columns, dims.block) for i in pair], axis=1
            )
            lanes = slice(k * dims.block, (k + len(pair)) * dims.block)
            out_ref[at(step, dims.chunk), lanes] = dot(hot, root).astype(BF16)

    repeat_steps(dims.chunks, body)


def plane_kernel(
    dims, sigma_ref, sigma2_ref, cols_ref, wgt_ref, nb_ref, obs_ref, plane_ref, opw_ref
):
    tile = lax.axis_index("space")
    half = lax.rem(lax.axis_index("var"), 2)
    bands = obs_ref.shape[0]
    flat = bands * dims.members
    shape = (dims.lanes, dims.vars)
    vars_wide = as_bf16(within(iota(shape, 0) - dims.members * iota(shape, 1), 0, dims.members))
    shape = (bands, flat)
    bands_wide = as_bf16(within(iota(shape, 1) - dims.members * iota(shape, 0), 0, dims.members))
    opw = dot(dot_nt(vars_wide, obs_ref[...]).astype(BF16), bands_wide)
    same = lax.rem(iota(opw.shape, 0), dims.members) == lax.rem(iota(opw.shape, 1), dims.members)
    opw_ref[...] = jnp.where(same, opw, 0.0).astype(BF16)
    sigma, sigma2 = sigma_ref[...], sigma2_ref[...]
    sigma = jnp.concatenate(
        [jnp.where(half == 0, sigma, sigma2), jnp.where(half == 0, sigma2, sigma)], axis=0
    )
    high = sigma.astype(BF16).astype(F32)
    nb = nb_ref[...] - (tile + partner_step(tile, half)) * dims.blocks
    nb = nb.astype(F32)
    base = 2 * dims.vars
    ids = jnp.zeros((dims.plane - base, dims.columns), F32)
    shape = ids.shape
    for b in range(dims.blocks):
        in_block = within(iota(shape, 1), b * dims.block, dims.block)
        for k in range(dims.others):
            ids = jnp.where(in_block & (iota(shape, 0) == k), nb[b : b + 1, k + 1 : k + 2], ids)
    rest = jnp.zeros_like(ids)
    table = jnp.concatenate([high, ids, sigma - high, rest], axis=0).astype(BF16)

    def body(step):
        points = at(step, dims.chunk_points)
        hot = one_hot(column(cols_ref[points, :]), dims.columns)
        plane = dot_nt(table, hot)
        scale = (plane[:base] + plane[dims.plane : dims.plane + base]) * row_of(wgt_ref[points, :])
        plane = jnp.concatenate([scale, plane[base : dims.plane]], axis=0).astype(BF16)
        plane_ref[:, at(step, dims.chunk)] = plane

    repeat_steps(dims.chunks, body)


def own_kernel(
    dims, roots_ref, cols_ref, rows_ref, plane_ref, control_ref, opw_ref, model_ref, opt_ref, op_ref
):
    half = lax.rem(lax.axis_index("var"), 2)
    opw = opw_ref[...]
    spread, targets_of = scale_spread(dims, half), target_spread(dims)
    root = roots_ref[:, 0].reshape(dims.columns, dims.block)
    shift = (partner_step(lax.axis_index("space"), half) * dims.blocks).astype(F32)

    def body(step):
        rows = at(step, dims.chunk)
        plane = plane_ref[:, rows].T
        cols = column(cols_ref[at(step, dims.chunk_points), :])
        own = jnp.floor(cols * (1.0 / dims.block))
        targets = [jnp.broadcast_to(own, (dims.chunk, dims.block)).astype(BF16)]
        parts = [dot(one_hot(cols, dims.columns), root).astype(BF16)]
        ids = (dot(plane, targets_of) + shift).astype(BF16)
        for k in range(dims.others):
            targets.append(ids[:, k * dims.block : (k + 1) * dims.block])
        parts += roots_of(dims, rows_ref, step)
        fill_operator(dims, op_ref, targets, parts)
        model = model_rows(dims, op_ref, dot(plane, spread), control_ref, opw)
        if isinstance(step, int) and step == 0:
            model_ref[...] = model
        else:
            model_ref[...] += model
        opt_ref[:, rows] = op_ref[...].T

    if dims.chunks > 2:
        model_ref[...] = jnp.zeros_like(model_ref)
    repeat_steps(dims.chunks, body)


def side_kernel(dims, rows_ref, plane_ref, control_ref, opw_ref, model_ref, op_ref):
    half = lax.rem(lax.axis_index("var"), 2)
    spread, targets_of = scale_spread(dims, half), target_spread(dims)
    opw = opw_ref[...]

    def body(step):
        plane = plane_ref[:, at(step, dims.chunk)].T
        ids = dot(plane, targets_of).astype(BF16)
        targets = [ids[:, k * dims.block : (k + 1) * dims.block] for k in range(dims.others)]
        fill_operator(dims, op_ref, targets, roots_of(dims, rows_ref, step))
        model = model_rows(dims, op_ref, dot(plane, spread), control_ref, opw)
        if isinstance(step, int) and step == 0:
            model_ref[...] = model
        else:
            model_ref[...] += model

    if dims.chunks > 2:
        model_ref[...] = jnp.zeros_like(model_ref)
    repeat_steps(dims.chunks, body)


def fill_turned(dims, opt_ref, rows_ref, plane_ref):
    def body(step):
        plane = plane_ref[:, at(step, dims.chunk)].astype(F32)
        parts = [part.T for part in roots_of(dims, rows_ref, step)]
        targets = []
        for k in range(dims.others):
            row = plane[2 * dims.vars + k : 2 * dims.vars + k + 1]
            targets.append(jnp.broadcast_to(row, (dims.block, dims.chunk)).astype(BF16))
        for q in range(dims.blocks):
            total = None
            for target, part in zip(targets, parts):
                term = jnp.where(target == jnp.asarray(q, BF16), part, jnp.zeros((), BF16))
                total = term if total is None else total + term
            opt_ref[q * dims.block : (q + 1) * dims.block, at(step, dims.chunk)] = total

    repeat_steps(dims.chunks, body)


def adjoint_kernel(
    dims, misfit_ref, plane_ref, opt_ref, base_ref, opw_ref, out_ref, adj_ref, finish=None
):
    half = lax.rem(lax.axis_index("var"), 2)
    spread = scale_spread(dims, half)
    misfit, opw = misfit_ref[...], opw_ref[...]
    high = misfit.astype(BF16)
    rest = misfit - high.astype(F32)
    middle = rest.astype(BF16)
    low = (rest - middle.astype(F32)).astype(BF16)
    pulled = dot_nt(high, opw) + (dot_nt(middle, opw) + dot_nt(low, opw))

    def body(step):
        scale = dot(plane_ref[:, at(step, dims.chunk)].T, spread)
        wide = scale.reshape(dims.chunk_points, dims.slots, dims.lanes) * pulled[None]
        adj_ref[at(step, dims.chunk), :] = wide.reshape(dims.chunk, dims.lanes).astype(BF16)

    repeat_steps(dims.chunks, body)
    for part in range(dims.columns // 256):
        rows = slice(part * 256, (part + 1) * 256)
        total = base_ref[rows, :].astype(F32) + dot(opt_ref[rows, :], adj_ref[...])
        out_ref[rows, :] = total.astype(out_ref.dtype)
        if finish is not None:
            finish(part, rows)


def side_adjoint_kernel(
    dims, misfit_ref, plane_ref, rows_ref, base_ref, opw_ref, out_ref, adj_ref, opt_ref
):
    fill_turned(dims, opt_ref, rows_ref, plane_ref)
    adjoint_kernel(dims, misfit_ref, plane_ref, opt_ref, base_ref, opw_ref, out_ref, adj_ref)


def last_adjoint_kernel(
    dims, misfit_ref, plane_ref, rows_ref, base_ref, opw_ref, out_hbm, adj_ref, opt_ref, out_ref, sems
):
    copies = []

    def finish(part, rows):
        copies.append(pltpu.make_async_copy(out_ref.at[rows], out_hbm.at[rows], sems.at[part]))
        copies[-1].start()

    fill_turned(dims, opt_ref, rows_ref, plane_ref)
    adjoint_kernel(
        dims, misfit_ref, plane_ref, opt_ref, base_ref, opw_ref, out_ref, adj_ref, finish
    )
    for copy in copies:
        copy.wait()


class Dims:
    def __init__(self, control, roots, sigma, foot_cols):
        self.blocks, links, self.block = roots.shape[:3]
        self.others = links - 1
        self.columns, self.lanes = control.shape
        self.vars = sigma.shape[0]
        self.members = self.lanes // self.vars
        self.slots, self.points = foot_cols.shape
        self.rows = self.slots * self.points
        self.chunk_points = min(self.points, max(8, 512 // self.slots))
        self.chunk = self.chunk_points * self.slots
        self.chunks = self.rows // self.chunk
        self.width = self.others * self.block
        self.plane = 64


def call(dims, kernel, name, out_shape, scratch, flops, out_specs=None):
    limit = min(56, max(16, dims.rows // 32)) * 1024 * 1024
    return pl.pallas_call(
        functools.partial(kernel, dims),
        out_shape=out_shape,
        scratch_shapes=scratch,
        compiler_params=pltpu.CompilerParams(vmem_limit_bytes=limit),
        cost_estimate=pl.CostEstimate(flops=flops, bytes_accessed=4000000, transcendentals=0),
        name=name,
        **({} if out_specs is None else {"out_specs": out_specs}),
    )


def shards(
    control,
    roots,
    neighbours,
    sigma,
    obs_op,
    foot_cols,
    foot_wgt,
    obs_value,
    obs_rinv,
    owner_counts,
):
    dims = Dims(control, roots, sigma, foot_cols)
    bands = obs_op.shape[1]
    members = dims.members
    tiles = lax.axis_size("space")
    ranks = lax.axis_size("var")
    partners = []
    for t in range(tiles):
        for v in range(ranks):
            to = t + (1 - 2 * (t % 2)) * (1 - 2 * (v % 2))
            if 0 <= to < tiles:
                partners.append((t * ranks + v, to * ranks + v))
    hop = lambda x: lax.ppermute(x, ("space", "var"), partners)
    swap = lambda x, bit: lax.ppermute(x, "var", [(i, i ^ bit) for i in range(ranks)])
    shape = jax.ShapeDtypeStruct
    flat = bands * members
    cols_t, wgt_t = foot_cols.T, foot_wgt.T

    sigma2 = swap(sigma, 1)
    picked = call(
        dims, select_kernel, "select", shape((dims.rows, dims.width), BF16), [], 2000000000
    )(roots, cols_t)
    mine = hop(picked)
    picked, sigma2 = lax.optimization_barrier((picked, sigma2))
    plane, opw = call(
        dims,
        plane_kernel,
        "plane",
        (shape((dims.plane, dims.rows), BF16), shape((dims.lanes, flat), BF16)),
        [],
        1000000000,
    )(sigma, sigma2, cols_t, wgt_t, neighbours, obs_op.T)
    mine_plane = hop(plane)
    plane, obs_value, obs_rinv, owner_counts = lax.optimization_barrier(
        (plane, obs_value, obs_rinv, owner_counts)
    )
    observed = lax.all_to_all(
        jnp.concatenate([obs_value, obs_rinv], axis=1), "space", 0, 0, tiled=True
    )
    capacity = dims.slots // owner_counts.shape[1]
    slot_ids = jnp.arange(dims.slots, dtype=jnp.int32)
    live = slot_ids % capacity < jnp.repeat(owner_counts[0], capacity)
    rinv = jnp.repeat(jnp.where(live[:, None], observed[:, flat:], 0.0), members, axis=1)
    value = observed[:, :flat]

    mine, mine_plane, rinv, value = lax.optimization_barrier((mine, mine_plane, rinv, value))
    other, other_plane = swap(mine, 1), swap(mine_plane, 1)
    op_scratch = [pltpu.VMEM((dims.chunk, dims.columns), BF16)]
    keep = call(
        dims, side_kernel, "mine_model", shape((dims.slots, flat), F32), op_scratch, 2000000000
    )(mine, mine_plane, control, opw)
    other, keep = lax.optimization_barrier((other, keep))
    give = call(
        dims, side_kernel, "other_model", shape((dims.slots, flat), F32), op_scratch, 2000000000
    )(other, other_plane, control, opw)
    arrived = hop(keep + swap(give, 1))
    give, own_picked = lax.optimization_barrier((give, picked))
    own_model, own_opt = call(
        dims,
        own_kernel,
        "own_model",
        (shape((dims.slots, flat), F32), shape((dims.columns, dims.rows), BF16)),
        op_scratch,
        4000000000,
    )(roots, cols_t, own_picked, plane, control, opw)
    arrived, own_model, own_opt = lax.optimization_barrier((arrived, own_model, own_opt))
    modelled = arrived + own_model
    bit = 1
    while bit < ranks:
        modelled = modelled + swap(modelled, bit)
        bit *= 2
    misfit = rinv * (modelled - value)
    misfit_mine = hop(misfit)

    def add_adjoint(kernel, name, dtype, scratch, *operands, out_specs=None):
        return call(
            dims,
            kernel,
            name,
            shape((dims.columns, dims.lanes), dtype),
            [pltpu.VMEM((dims.rows, dims.lanes), BF16)] + scratch,
            2000000000,
            out_specs,
        )(*operands, opw)

    total = add_adjoint(
        adjoint_kernel, "own_adjoint", F32, [], misfit, plane, own_opt, control
    )
    misfit_mine, total = lax.optimization_barrier((misfit_mine, total))
    misfit_other = swap(misfit_mine, 1)
    turned = [pltpu.VMEM((dims.columns, dims.rows), BF16)]
    total = add_adjoint(
        side_adjoint_kernel, "mine_adjoint", F32, turned, misfit_mine, mine_plane, mine, total
    )
    misfit_other, total = lax.optimization_barrier((misfit_other, total))
    sent = [
        pltpu.VMEM((dims.columns, dims.lanes), BF16),
        pltpu.SemaphoreType.DMA((dims.columns // 256,)),
    ]
    return add_adjoint(
        last_adjoint_kernel, "other_adjoint", BF16, turned + sent,
        misfit_other, other_plane, other, total, out_specs=pl.BlockSpec(memory_space=pl.ANY),
    )


def solution(mesh):
    return jax.shard_map(
        shards,
        mesh=mesh,
        in_specs=(
            P("space", "var"),
            P("space", None, None, None),
            P("space", None),
            P("var", "space"),
            P("var", None),
            P("space", None),
            P("space", None),
            P("space", None),
            P("space", None),
            P("space", None),
        ),
        out_specs=P("space", "var"),
        check_vma=False,
    )
```

```python
import functools

import jax
import jax.numpy as jnp
from jax import lax
from jax.experimental import pallas as pl
from jax.experimental.pallas import tpu as pltpu
from jax.sharding import PartitionSpec as P

F32 = jnp.float32
BF16 = jnp.bfloat16
NT = (((1,), (1,)), ((), ()))


def repeat_steps(count, body):
    if count <= 2:
        for step in range(count):
            body(step)
    else:
        lax.fori_loop(0, count, lambda step, carry: (body(step), carry)[1], 0)


def at(step, size):
    if isinstance(step, int):
        return pl.ds(step * size, size)
    return pl.ds(pl.multiple_of(step * size, size), size)


def dot(a, b):
    return jnp.dot(a, b, preferred_element_type=F32)


def dot_nt(a, b):
    return lax.dot_general(a, b, NT, preferred_element_type=F32)


def iota(shape, axis):
    return lax.broadcasted_iota(jnp.int32, shape, axis)


def spread_rows(values):
    points, slots = values.shape
    wide = jnp.broadcast_to(values.astype(F32)[:, None, :], (points, slots, slots))
    wide = wide.reshape(points * slots, slots)
    hit = iota(wide.shape, 1) == lax.rem(iota(wide.shape, 0), slots)
    return jnp.where(hit, wide, 0.0)


def column(values):
    return jnp.sum(spread_rows(values), axis=1, keepdims=True)


def row_of(values):
    wide = spread_rows(values)
    high = wide.astype(BF16)
    low = (wide - high.astype(F32)).astype(BF16)
    ones = jnp.ones((8, wide.shape[1]), BF16)
    return (dot_nt(ones, high) + dot_nt(ones, low))[:1]


def one_hot(cols, count):
    lane = iota((cols.shape[0], count), 1)
    return jnp.where(lane == cols.astype(jnp.int32), 1.0, 0.0).astype(BF16)


def within(value, low, count):
    return (value >= low) & (value < low + count)


def as_bf16(mask):
    return jnp.where(mask, 1.0, 0.0).astype(BF16)


def scale_spread(dims, half):
    shape = (dims.plane, dims.lanes)
    row = iota(shape, 0) - dims.vars * half
    return as_bf16(within(iota(shape, 1) - dims.members * row, 0, dims.members))


def target_spread(dims):
    shape = (dims.plane, dims.width)
    row = iota(shape, 0) - 2 * dims.vars
    return as_bf16(within(iota(shape, 1) - dims.block * row, 0, dims.block))


def roots_of(dims, rows_ref, step):
    rows = at(step, dims.chunk)
    return [rows_ref[rows, k * dims.block : (k + 1) * dims.block] for k in range(dims.others)]


def fill_operator(dims, op_ref, targets, parts):
    for q in range(dims.blocks):
        total = None
        for target, part in zip(targets, parts):
            term = jnp.where(target == jnp.asarray(q, target.dtype), part, jnp.zeros((), part.dtype))
            total = term if total is None else total + term
        op_ref[:, q * dims.block : (q + 1) * dims.block] = total


def model_rows(dims, op_ref, scale, control_ref, opw):
    summed = dot(op_ref[...], control_ref[...])
    state = (summed * scale).astype(BF16)
    bands = dot(state, opw)
    return jnp.sum(bands.reshape(dims.chunk_points, dims.slots, bands.shape[1]), axis=0)


def partner_step(tile, rank):
    return (1 - 2 * lax.rem(tile, 2)) * (1 - 2 * lax.rem(rank, 2))


def select_kernel(dims, roots_ref, cols_ref, out_ref):
    def body(step):
        hot = one_hot(column(cols_ref[at(step, dims.chunk_points), :]), dims.columns)
        for k in range(0, dims.others, 2):
            pair = range(k, min(k + 2, dims.others))
            root = jnp.concatenate(
                [roots_ref[:, i + 1].reshape(dims.columns, dims.block) for i in pair], axis=1
            )
            lanes = slice(k * dims.block, (k + len(pair)) * dims.block)
            out_ref[at(step, dims.chunk), lanes] = dot(hot, root).astype(BF16)

    repeat_steps(dims.chunks, body)


def plane_kernel(
    dims, sigma_ref, sigma2_ref, cols_ref, wgt_ref, nb_ref, obs_ref, plane_ref, opw_ref
):
    tile = lax.axis_index("space")
    half = lax.rem(lax.axis_index("var"), 2)
    bands = obs_ref.shape[0]
    flat = bands * dims.members
    shape = (dims.lanes, dims.vars)
    vars_wide = as_bf16(within(iota(shape, 0) - dims.members * iota(shape, 1), 0, dims.members))
    shape = (bands, flat)
    bands_wide = as_bf16(within(iota(shape, 1) - dims.members * iota(shape, 0), 0, dims.members))
    opw = dot(dot_nt(vars_wide, obs_ref[...]).astype(BF16), bands_wide)
    same = lax.rem(iota(opw.shape, 0), dims.members) == lax.rem(iota(opw.shape, 1), dims.members)
    opw_ref[...] = jnp.where(same, opw, 0.0).astype(BF16)
    sigma, sigma2 = sigma_ref[...], sigma2_ref[...]
    sigma = jnp.concatenate(
        [jnp.where(half == 0, sigma, sigma2), jnp.where(half == 0, sigma2, sigma)], axis=0
    )
    high = sigma.astype(BF16).astype(F32)
    nb = nb_ref[...] - (tile + partner_step(tile, half)) * dims.blocks
    nb = nb.astype(F32)
    base = 2 * dims.vars
    ids = jnp.zeros((dims.plane - base, dims.columns), F32)
    shape = ids.shape
    for b in range(dims.blocks):
        in_block = within(iota(shape, 1), b * dims.block, dims.block)
        for k in range(dims.others):
            ids = jnp.where(in_block & (iota(shape, 0) == k), nb[b : b + 1, k + 1 : k + 2], ids)
    rest = jnp.zeros_like(ids)
    table = jnp.concatenate([high, ids, sigma - high, rest], axis=0).astype(BF16)

    def body(step):
        points = at(step, dims.chunk_points)
        hot = one_hot(column(cols_ref[points, :]), dims.columns)
        plane = dot_nt(table, hot)
        scale = (plane[:base] + plane[dims.plane : dims.plane + base]) * row_of(wgt_ref[points, :])
        plane = jnp.concatenate([scale, plane[base : dims.plane]], axis=0).astype(BF16)
        plane_ref[:, at(step, dims.chunk)] = plane

    repeat_steps(dims.chunks, body)


def own_kernel(
    dims, roots_ref, cols_ref, rows_ref, plane_ref, control_ref, opw_ref, model_ref, opt_ref, op_ref
):
    half = lax.rem(lax.axis_index("var"), 2)
    opw = opw_ref[...]
    spread, targets_of = scale_spread(dims, half), target_spread(dims)
    root = roots_ref[:, 0].reshape(dims.columns, dims.block)
    shift = (partner_step(lax.axis_index("space"), half) * dims.blocks).astype(F32)

    def body(step):
        rows = at(step, dims.chunk)
        plane = plane_ref[:, rows].T
        cols = column(cols_ref[at(step, dims.chunk_points), :])
        own = jnp.floor(cols * (1.0 / dims.block))
        targets = [jnp.broadcast_to(own, (dims.chunk, dims.block)).astype(BF16)]
        parts = [dot(one_hot(cols, dims.columns), root).astype(BF16)]
        ids = (dot(plane, targets_of) + shift).astype(BF16)
        for k in range(dims.others):
            targets.append(ids[:, k * dims.block : (k + 1) * dims.block])
        parts += roots_of(dims, rows_ref, step)
        fill_operator(dims, op_ref, targets, parts)
        model = model_rows(dims, op_ref, dot(plane, spread), control_ref, opw)
        if isinstance(step, int) and step == 0:
            model_ref[...] = model
        else:
            model_ref[...] += model
        opt_ref[:, rows] = op_ref[...].T

    if dims.chunks > 2:
        model_ref[...] = jnp.zeros_like(model_ref)
    repeat_steps(dims.chunks, body)


def side_kernel(dims, rows_ref, plane_ref, control_ref, opw_ref, model_ref, op_ref):
    half = lax.rem(lax.axis_index("var"), 2)
    spread, targets_of = scale_spread(dims, half), target_spread(dims)
    opw = opw_ref[...]

    def body(step):
        plane = plane_ref[:, at(step, dims.chunk)].T
        ids = dot(plane, targets_of).astype(BF16)
        targets = [ids[:, k * dims.block : (k + 1) * dims.block] for k in range(dims.others)]
        fill_operator(dims, op_ref, targets, roots_of(dims, rows_ref, step))
        model = model_rows(dims, op_ref, dot(plane, spread), control_ref, opw)
        if isinstance(step, int) and step == 0:
            model_ref[...] = model
        else:
            model_ref[...] += model

    if dims.chunks > 2:
        model_ref[...] = jnp.zeros_like(model_ref)
    repeat_steps(dims.chunks, body)


def fill_turned(dims, opt_ref, rows_ref, plane_ref):
    def body(step):
        plane = plane_ref[:, at(step, dims.chunk)].astype(F32)
        parts = [part.T for part in roots_of(dims, rows_ref, step)]
        targets = []
        for k in range(dims.others):
            row = plane[2 * dims.vars + k : 2 * dims.vars + k + 1]
            targets.append(jnp.broadcast_to(row, (dims.block, dims.chunk)).astype(BF16))
        for q in range(dims.blocks):
            total = None
            for target, part in zip(targets, parts):
                term = jnp.where(target == jnp.asarray(q, BF16), part, jnp.zeros((), BF16))
                total = term if total is None else total + term
            opt_ref[q * dims.block : (q + 1) * dims.block, at(step, dims.chunk)] = total

    repeat_steps(dims.chunks, body)


def adjoint_kernel(
    dims, misfit_ref, plane_ref, opt_ref, base_ref, opw_ref, out_ref, adj_ref, finish=None
):
    half = lax.rem(lax.axis_index("var"), 2)
    spread = scale_spread(dims, half)
    misfit, opw = misfit_ref[...], opw_ref[...]
    high = misfit.astype(BF16)
    rest = misfit - high.astype(F32)
    middle = rest.astype(BF16)
    low = (rest - middle.astype(F32)).astype(BF16)
    pulled = dot_nt(high, opw) + (dot_nt(middle, opw) + dot_nt(low, opw))

    def body(step):
        scale = dot(plane_ref[:, at(step, dims.chunk)].T, spread)
        wide = scale.reshape(dims.chunk_points, dims.slots, dims.lanes) * pulled[None]
        adj_ref[at(step, dims.chunk), :] = wide.reshape(dims.chunk, dims.lanes).astype(BF16)

    repeat_steps(dims.chunks, body)
    for part in range(dims.columns // 256):
        rows = slice(part * 256, (part + 1) * 256)
        total = base_ref[rows, :].astype(F32) + dot(opt_ref[rows, :], adj_ref[...])
        out_ref[rows, :] = total.astype(out_ref.dtype)
        if finish is not None:
            finish(part, rows)


def side_adjoint_kernel(
    dims, misfit_ref, plane_ref, rows_ref, base_ref, opw_ref, out_ref, adj_ref, opt_ref
):
    fill_turned(dims, opt_ref, rows_ref, plane_ref)
    adjoint_kernel(dims, misfit_ref, plane_ref, opt_ref, base_ref, opw_ref, out_ref, adj_ref)


def last_adjoint_kernel(
    dims, misfit_ref, plane_ref, rows_ref, base_ref, opw_ref, out_hbm, adj_ref, opt_ref, out_ref, sems
):
    copies = []

    def finish(part, rows):
        copies.append(pltpu.make_async_copy(out_ref.at[rows], out_hbm.at[rows], sems.at[part]))
        copies[-1].start()

    fill_turned(dims, opt_ref, rows_ref, plane_ref)
    adjoint_kernel(
        dims, misfit_ref, plane_ref, opt_ref, base_ref, opw_ref, out_ref, adj_ref, finish
    )
    for copy in copies:
        copy.wait()


class Dims:
    def __init__(self, control, roots, sigma, foot_cols):
        self.blocks, links, self.block = roots.shape[:3]
        self.others = links - 1
        self.columns, self.lanes = control.shape
        self.vars = sigma.shape[0]
        self.members = self.lanes // self.vars
        self.slots, self.points = foot_cols.shape
        self.rows = self.slots * self.points
        self.chunk_points = min(self.points, max(8, 512 // self.slots))
        self.chunk = self.chunk_points * self.slots
        self.chunks = self.rows // self.chunk
        self.width = self.others * self.block
        self.plane = 64


def call(dims, kernel, name, out_shape, scratch, flops, out_specs=None):
    limit = min(56, max(16, dims.rows // 32)) * 1024 * 1024
    return pl.pallas_call(
        functools.partial(kernel, dims),
        out_shape=out_shape,
        scratch_shapes=scratch,
        compiler_params=pltpu.CompilerParams(vmem_limit_bytes=limit),
        cost_estimate=pl.CostEstimate(flops=flops, bytes_accessed=4000000, transcendentals=0),
        name=name,
        **({} if out_specs is None else {"out_specs": out_specs}),
    )


def shards(
    control,
    roots,
    neighbours,
    sigma,
    obs_op,
    foot_cols,
    foot_wgt,
    obs_value,
    obs_rinv,
    owner_counts,
):
    dims = Dims(control, roots, sigma, foot_cols)
    bands = obs_op.shape[1]
    members = dims.members
    tiles = lax.axis_size("space")
    ranks = lax.axis_size("var")
    partners = []
    for t in range(tiles):
        for v in range(ranks):
            to = t + (1 - 2 * (t % 2)) * (1 - 2 * (v % 2))
            if 0 <= to < tiles:
                partners.append((t * ranks + v, to * ranks + v))
    hop = lambda x: lax.ppermute(x, ("space", "var"), partners)
    swap = lambda x, bit: lax.ppermute(x, "var", [(i, i ^ bit) for i in range(ranks)])
    shape = jax.ShapeDtypeStruct
    flat = bands * members
    cols_t, wgt_t = foot_cols.T, foot_wgt.T

    sigma2 = swap(sigma, 1)
    picked = call(
        dims, select_kernel, "select", shape((dims.rows, dims.width), BF16), [], 2000000000
    )(roots, cols_t)
    picked, sigma2 = lax.optimization_barrier((picked, sigma2))
    mine = hop(picked)
    plane, opw = call(
        dims,
        plane_kernel,
        "plane",
        (shape((dims.plane, dims.rows), BF16), shape((dims.lanes, flat), BF16)),
        [],
        1000000000,
    )(sigma, sigma2, cols_t, wgt_t, neighbours, obs_op.T)
    mine_plane = hop(plane)
    plane, obs_value, obs_rinv, owner_counts = lax.optimization_barrier(
        (plane, obs_value, obs_rinv, owner_counts)
    )
    observed = lax.all_to_all(
        jnp.concatenate([obs_value, obs_rinv], axis=1), "space", 0, 0, tiled=True
    )
    capacity = dims.slots // owner_counts.shape[1]
    slot_ids = jnp.arange(dims.slots, dtype=jnp.int32)
    live = slot_ids % capacity < jnp.repeat(owner_counts[0], capacity)
    rinv = jnp.repeat(jnp.where(live[:, None], observed[:, flat:], 0.0), members, axis=1)
    value = observed[:, :flat]

    other, other_plane = swap(mine, 1), swap(mine_plane, 1)
    op_scratch = [pltpu.VMEM((dims.chunk, dims.columns), BF16)]
    keep = call(
        dims, side_kernel, "mine_model", shape((dims.slots, flat), F32), op_scratch, 2000000000
    )(mine, mine_plane, control, opw)
    other, keep, rinv, value = lax.optimization_barrier((other, keep, rinv, value))
    give = call(
        dims, side_kernel, "other_model", shape((dims.slots, flat), F32), op_scratch, 2000000000
    )(other, other_plane, control, opw)
    arrived = hop(keep + swap(give, 1))
    give, own_picked = lax.optimization_barrier((give, picked))
    own_model, own_opt = call(
        dims,
        own_kernel,
        "own_model",
        (shape((dims.slots, flat), F32), shape((dims.columns, dims.rows), BF16)),
        op_scratch,
        4000000000,
    )(roots, cols_t, own_picked, plane, control, opw)
    arrived, own_model, own_opt = lax.optimization_barrier((arrived, own_model, own_opt))
    modelled = arrived + own_model
    bit = 1
    while bit < ranks:
        modelled = modelled + swap(modelled, bit)
        bit *= 2
    misfit = rinv * (modelled - value)
    misfit_mine = hop(misfit)

    def add_adjoint(kernel, name, dtype, scratch, *operands, out_specs=None):
        return call(
            dims,
            kernel,
            name,
            shape((dims.columns, dims.lanes), dtype),
            [pltpu.VMEM((dims.rows, dims.lanes), BF16)] + scratch,
            2000000000,
            out_specs,
        )(*operands, opw)

    total = add_adjoint(
        adjoint_kernel, "own_adjoint", F32, [], misfit, plane, own_opt, control
    )
    misfit_mine, total = lax.optimization_barrier((misfit_mine, total))
    misfit_other = swap(misfit_mine, 1)
    turned = [pltpu.VMEM((dims.columns, dims.rows), BF16)]
    total = add_adjoint(
        side_adjoint_kernel, "mine_adjoint", F32, turned, misfit_mine, mine_plane, mine, total
    )
    misfit_other, total = lax.optimization_barrier((misfit_other, total))
    sent = [
        pltpu.VMEM((dims.columns, dims.lanes), BF16),
        pltpu.SemaphoreType.DMA((dims.columns // 256,)),
    ]
    return add_adjoint(
        last_adjoint_kernel, "other_adjoint", BF16, turned + sent,
        misfit_other, other_plane, other, total, out_specs=pl.BlockSpec(memory_space=pl.ANY),
    )


def solution(mesh):
    return jax.shard_map(
        shards,
        mesh=mesh,
        in_specs=(
            P("space", "var"),
            P("space", None, None, None),
            P("space", None),
            P("var", "space"),
            P("var", None),
            P("space", None),
            P("space", None),
            P("space", None),
            P("space", None),
            P("space", None),
        ),
        out_specs=P("space", "var"),
        check_vma=False,
    )
```
